256 devices in a mesh: dp: 32 (over x, z), tensor: 8 (over y, core).
Axes of the slice: x: 4, y: 4, z: 8, core: 2. Of those that a mesh axis runs over, the one named last changes fastest.
Arguments:
- ssm_resident: bfloat16 [256, 64, 64, 256], P('dp', 'tensor'), may hold values from -6 to 6
- ssm_nodes: bfloat16 [128, 64, 64, 256], P('dp', 'tensor'), may hold values from -6 to 6
- conv_resident: bfloat16 [256, 3, 4096], P('dp', None, 'tensor'), may hold values from -6 to 6
- conv_nodes: bfloat16 [128, 3, 4096], P('dp', None, 'tensor'), may hold values from -6 to 6
- convbc_resident: bfloat16 [256, 3, 512], P('dp'), may hold values from -6 to 6
- convbc_nodes: bfloat16 [128, 3, 512], P('dp'), may hold values from -6 to 6
- kv_resident: bfloat16 [256, 2, 256, 1024], P('dp', None, None, 'tensor'), may hold values from -6 to 6
- kv_nodes: bfloat16 [128, 2, 256, 1024], P('dp', None, None, 'tensor'), may hold values from -6 to 6
- len_resident: int32 [256], P('dp'), may hold values from 1 to 256, as said below
- len_nodes: int32 [128], replicated, may hold values from 1 to 256, as said below
- parents: int32 [512], replicated, may hold values from 0 to 127, as said below
- alive_flags: int32 [768], P('dp'), may hold values 0 or 1
- queries: bfloat16 [768, 4, 5120], P('dp', None, 'tensor'), may hold values from -120 to 120
- new_kv: bfloat16 [768, 2, 4, 1024], P('dp', None, None, 'tensor'), may hold values from -6 to 6
- x_in: bfloat16 [768, 4, 4096], P('dp', None, 'tensor'), may hold values from -6 to 6
- gate_in: bfloat16 [768, 4, 4096], P('dp', None, 'tensor'), may hold values from -6 to 6
- bc_in: bfloat16 [768, 4, 512], P('dp'), may hold values from -6 to 6
- dt_in: bfloat16 [768, 4, 64], P('dp', None, 'tensor'), may hold values from -4 to 4
- conv_x_weight: bfloat16 [4, 4096], P(None, 'tensor'), may hold values from -3 to 3
- conv_bc_weight: bfloat16 [4, 512], replicated, may hold values from -3 to 3
- a_log: float32 [64], P('tensor'), may hold values from -4 to 0.5
- dt_bias: float32 [64], P('tensor'), may hold values from -2 to 0.5
- skip_gain: float32 [64], P('tensor'), may hold values from 0.5 to 2
- norm_gain: float32 [4096], P('tensor'), may hold values from 0.5 to 1.5
Outputs:
- attn_out: bfloat16 [768, 4, 5120], P('dp', None, 'tensor')
- ssm_out: bfloat16 [768, 4, 4096], P('dp', None, 'tensor')
- new_ssm: bfloat16 [768, 64, 64, 256], P('dp', 'tensor')
The draws below stay inside these ranges and needn't reach their ends.
Inputs may be any that keep to these rules, and one draw needn't show every extreme that they name: Node n is stored on index n // 4 of dp. The child rows of one index of dp take parents from exactly 12 indices of dp, or from all indices where dp has fewer than 12; those with parents on the same index share one parent and number at most 2, a number reached on every index. `len_resident`: every block of 8 rows of one index of dp holds a row of length 256. `len_nodes`: every block of 4 nodes of one index of dp holds a node of length 256.
All inputs are finite; a program needn't handle non-finite values. No bound on the sum of `alive_flags` on one device may be relied on, other than what follows from the above.
Results may differ from the reference program's by a relative error of at most 0.002.
Values may be sent and summed in bfloat16 or wider, within the bound.
A program may use at most 128 MiB of HBM per device.

```python
import jax
import jax.numpy as jnp
from jax import lax

ATT_HEADS = 40
KV_HEADS = 8
HEAD = 128
SSM_HEADS = 64
SSM_HEAD = 64
STATE = 256
KERNEL = 4
STEPS = 4
CACHE = 256
RES_DEV = 8
CHILD_DEV = 16
NODE_DEV = 4
ROW_DEV = 24
ROWS = 768
RESIDENT = 256
CHILDREN = 512
NODES = 128
QW = 5120
KVW = 1024
INNER = 4096
BCW = 512


def tree_parents(key):
    key = jax.random.fold_in(key, 11)
    groups = CHILDREN // CHILD_DEV
    source_count = min(12, groups)

    def one_group(group_key):
        first, second, third, fourth = jax.random.split(group_key, 4)
        sources = jax.random.permutation(first, groups)[:source_count]
        extra = jax.random.permutation(second, source_count)[:CHILD_DEV - source_count]
        spots = jnp.concatenate([jnp.arange(source_count), extra], 0)
        spots = jax.random.permutation(fourth, spots)
        slot_picks = jax.random.randint(third, (source_count,), 0, NODE_DEV)
        return (sources * NODE_DEV + slot_picks)[spots]
    picked = jax.vmap(one_group)(jax.random.split(key, groups))
    return picked.reshape(CHILDREN).astype(jnp.int32)


def first_keys(key, salt_value, row_count):
    drawn = jax.random.normal(jax.random.fold_in(key, salt_value + 500), (row_count, KVW), jnp.float32)
    return jnp.clip(drawn, -6.0, 6.0)


def cache_block(key, salt_value, row_count):
    drawn_block = jax.random.normal(jax.random.fold_in(key, salt_value), (row_count, 2, CACHE, KVW), jnp.float32)
    drawn_block = jnp.clip(drawn_block, -6.0, 6.0)
    lead_keys = first_keys(key, salt_value, row_count)
    drawn_block = drawn_block.at[:, 0, 0].set(lead_keys)
    drawn_block = drawn_block.at[:, 0, 1].set(drawn_block[:, 0, 1])
    return drawn_block


def lengths_of(key, salt_value, row_count, block_rows):
    key = jax.random.fold_in(key, salt_value)
    first, second = jax.random.split(key)
    drawn_lengths = jax.random.randint(first, (row_count,), 1, CACHE + 1)
    full_slot = jax.random.randint(second, (row_count // block_rows,), 0, block_rows)
    is_full = jnp.arange(row_count) % block_rows == jnp.repeat(full_slot, block_rows)
    return jnp.where(is_full, CACHE, drawn_lengths).astype(jnp.int32)


def draw_parents(key, part):
    return tree_parents(key)


def draw_len_resident(key, part):
    return lengths_of(key, 41, RESIDENT, RES_DEV)


def draw_len_nodes(key, part):
    return lengths_of(key, 42, NODES, NODE_DEV)


def draw_kv_resident(key, part):
    return cache_block(key, 21, RESIDENT).astype(jnp.bfloat16)


def draw_kv_nodes(key, part):
    return cache_block(key, 22, NODES).astype(jnp.bfloat16)


def draw_queries(key, part):
    own_key = jax.random.fold_in(key, 31)
    drawn = jnp.clip(jax.random.normal(own_key, (ROWS, STEPS, QW), jnp.float32), -6.0, 6.0)
    return drawn.astype(jnp.bfloat16)


def touch_ends(values, key, least, top_value):
    extent = values.shape
    place = [jax.random.randint(jax.random.fold_in(key, axis), (), 0, extent[axis]) for axis in range(len(extent))]
    values = values.at[tuple(place)].set(least)
    longest = extent.index(max(extent))
    place[longest] = (place[longest] + 1) % extent[longest]
    return values.at[tuple(place)].set(top_value)


def level_of(stream_key, extent, shards, least, largest):
    factor_of = 1.0
    for position, blocks in shards:
        draws = jax.random.uniform(jax.random.fold_in(jax.random.fold_in(stream_key, 6), position), (blocks,), jnp.float32, least / len(shards), largest / len(shards))
        factor_of = factor_of * jnp.repeat(jnp.exp(draws), extent[position] // blocks).reshape((-1,) + (1,) * (len(extent) - 1 - position))
    return factor_of


def centred(key, extent, deviation, bound, pieces=(), kind=jnp.bfloat16):
    result = jax.random.normal(key, extent, jnp.float32) * deviation
    if len(pieces) > 0:
        result = level_of(key, extent, pieces, -0.22, 0.18) * result
    return jnp.clip(result, min=-bound, max=bound).astype(kind)


def setup_inputs(seed: int = 0) -> dict:
    streams_of = jax.random.split(jax.random.key(seed), 25)
    ssm_resident = centred(streams_of[0], (RESIDENT, SSM_HEADS, SSM_HEAD, STATE), 1.0, 6.0, ((0, 32), (1, 8)))
    ssm_nodes = centred(streams_of[1], (NODES, SSM_HEADS, SSM_HEAD, STATE), 1.0, 6.0, ((0, 32), (1, 8)))
    conv_resident = centred(streams_of[2], (RESIDENT, KERNEL - 1, INNER), 1.0, 6.0, ((0, 32), (2, 8)))
    conv_nodes = centred(streams_of[3], (NODES, KERNEL - 1, INNER), 1.0, 6.0, ((0, 32), (2, 8)))
    convbc_resident = centred(streams_of[4], (RESIDENT, KERNEL - 1, BCW), 1.0, 6.0, ((0, 32),))
    convbc_nodes = centred(streams_of[5], (NODES, KERNEL - 1, BCW), 1.0, 6.0, ((0, 32),))
    kv_resident = draw_kv_resident(jax.random.fold_in(streams_of[24], 71), 0)
    kv_nodes = draw_kv_nodes(jax.random.fold_in(streams_of[24], 71), 0)
    len_resident = draw_len_resident(jax.random.fold_in(streams_of[24], 71), 0)
    len_nodes = draw_len_nodes(jax.random.fold_in(streams_of[24], 71), 0)
    parents = draw_parents(jax.random.fold_in(streams_of[24], 71), 0)
    alive_flags = touch_ends((jax.random.randint(streams_of[11], (ROWS,), 0, 4) < 3).astype(jnp.int32), jax.random.fold_in(streams_of[11], 1), 0, 1)
    queries = draw_queries(jax.random.fold_in(streams_of[24], 71), 0)
    new_kv = centred(streams_of[13], (ROWS, 2, STEPS, KVW), 1.0, 6.0, ((0, 32), (3, 8)))
    x_in = centred(streams_of[14], (ROWS, STEPS, INNER), 1.0, 6.0, ((0, 32), (2, 8)))
    gate_in = centred(streams_of[15], (ROWS, STEPS, INNER), 1.0, 6.0, ((0, 32), (2, 8)))
    bc_in = centred(streams_of[16], (ROWS, STEPS, BCW), 1.0, 6.0, ((0, 32),))
    dt_in = centred(streams_of[17], (ROWS, STEPS, SSM_HEADS), 1.0, 4.0, ((0, 32), (2, 8)))
    conv_x_weight = centred(streams_of[18], (KERNEL, INNER), KERNEL ** -0.5, 3.0, ((1, 8),))
    conv_bc_weight = centred(streams_of[19], (KERNEL, BCW), KERNEL ** -0.5, 3.0)
    a_log = jnp.clip(-4.0 + 4.5 * jax.random.uniform(streams_of[20], (SSM_HEADS,), jnp.float32) ** level_of(streams_of[20], (SSM_HEADS,), ((0, 8),), -0.2, 0.2), -4.0, 0.5)
    dt_bias = jnp.clip(-2.0 + 2.5 * jax.random.uniform(streams_of[21], (SSM_HEADS,), jnp.float32) ** level_of(streams_of[21], (SSM_HEADS,), ((0, 8),), -0.2, 0.2), -2.0, 0.5)
    skip_gain = jnp.clip(0.5 + 1.5 * jax.random.uniform(streams_of[22], (SSM_HEADS,), jnp.float32) ** level_of(streams_of[22], (SSM_HEADS,), ((0, 8),), -0.2, 0.2), 0.5, 2.0)
    norm_gain = jnp.clip(1.0 + 0.1 * jax.random.normal(streams_of[23], (INNER,), jnp.float32), 0.5, 1.5)
    return {"ssm_resident": ssm_resident, "ssm_nodes": ssm_nodes, "conv_resident": conv_resident, "conv_nodes": conv_nodes, "convbc_resident": convbc_resident, "convbc_nodes": convbc_nodes, "kv_resident": kv_resident, "kv_nodes": kv_nodes, "len_resident": len_resident, "len_nodes": len_nodes, "parents": parents, "alive_flags": alive_flags, "queries": queries, "new_kv": new_kv, "x_in": x_in, "gate_in": gate_in, "bc_in": bc_in, "dt_in": dt_in, "conv_x_weight": conv_x_weight, "conv_bc_weight": conv_bc_weight, "a_log": a_log, "dt_bias": dt_bias, "skip_gain": skip_gain, "norm_gain": norm_gain}


EPSILON = 1e-05

def reference(ssm_resident, ssm_nodes, conv_resident, conv_nodes, convbc_resident, convbc_nodes, kv_resident, kv_nodes, len_resident, len_nodes, parents, alive_flags, queries, new_kv, x_in, gate_in, bc_in, dt_in, conv_x_weight, conv_bc_weight, a_log, dt_bias, skip_gain, norm_gain):
    group_heads = ATT_HEADS // KV_HEADS
    precise = lax.Precision.HIGHEST
    decay_rate = jnp.exp(a_log)

    def one_row(row_index):
        device_group = row_index // ROW_DEV
        inside = row_index % ROW_DEV
        is_child = inside >= RES_DEV
        resident_index = jnp.clip(device_group * RES_DEV + inside, 0, RESIDENT - 1).astype(jnp.int32)
        child_index = jnp.clip(device_group * CHILD_DEV + inside - RES_DEV, 0, CHILDREN - 1).astype(jnp.int32)
        parent_node = parents[child_index]

        def choose(resident, node_rows):
            return jnp.where(is_child, node_rows[parent_node], resident[resident_index])
        carry_state = choose(ssm_resident, ssm_nodes).astype(jnp.float32)
        conv_state = choose(conv_resident, conv_nodes).astype(jnp.float32)
        convbc_state = choose(convbc_resident, convbc_nodes).astype(jnp.float32)
        row_cache = choose(kv_resident, kv_nodes)
        length = choose(len_resident, len_nodes)
        conv_input = jnp.concatenate([conv_state, x_in[row_index].astype(jnp.float32)], 0)
        conv_bc_input = jnp.concatenate([convbc_state, bc_in[row_index].astype(jnp.float32)], 0)
        mixed_x = jnp.zeros((STEPS, INNER), jnp.float32)
        mixed_bc = jnp.zeros((STEPS, BCW), jnp.float32)
        for tap_index in range(KERNEL):
            mixed_x = mixed_x + conv_x_weight[tap_index].astype(jnp.float32) * conv_input[tap_index:tap_index + STEPS]
            mixed_bc = mixed_bc + conv_bc_weight[tap_index].astype(jnp.float32) * conv_bc_input[tap_index:tap_index + STEPS]
        mixed_x = jax.nn.silu(mixed_x)
        mixed_bc = jax.nn.silu(mixed_bc)
        b_part = mixed_bc[:, :STATE]
        c_part = mixed_bc[:, STATE:]
        dt_row = jax.nn.softplus(dt_in[row_index].astype(jnp.float32) + dt_bias)
        decay_step = jnp.exp(-decay_rate * dt_row)
        x_heads = mixed_x.reshape(STEPS, SSM_HEADS, SSM_HEAD)
        readouts = []
        for t in range(STEPS):
            carry_state = decay_step[t][:, None, None] * carry_state + (dt_row[t][:, None] * x_heads[t])[:, :, None] * b_part[t][None, None, :]
            readout = jnp.einsum('hpn,n->hp', carry_state, c_part[t], precision=precise) + skip_gain[:, None] * x_heads[t]
            readouts.append(readout.reshape(INNER))
        ssm_y = jnp.stack(readouts, 0)
        gated_out = ssm_y * jax.nn.silu(gate_in[row_index].astype(jnp.float32))
        mean_square = lax.optimization_barrier(jnp.sum(gated_out * gated_out, -1)) / INNER
        ssm_row = gated_out * lax.rsqrt(mean_square + EPSILON)[:, None] * norm_gain
        query_heads = queries[row_index].astype(jnp.float32).reshape(STEPS, KV_HEADS, group_heads, HEAD)
        cache_keys = row_cache[0].astype(jnp.float32).reshape(CACHE, KV_HEADS, HEAD)
        cache_values = row_cache[1].astype(jnp.float32).reshape(CACHE, KV_HEADS, HEAD)
        new_keys = new_kv[row_index, 0].astype(jnp.float32).reshape(STEPS, KV_HEADS, HEAD)
        new_values = new_kv[row_index, 1].astype(jnp.float32).reshape(STEPS, KV_HEADS, HEAD)
        cache_scores = jnp.einsum('thgc,nhc->thgn', query_heads, cache_keys, precision=precise) * HEAD ** (-0.5)
        cache_scores = jnp.where((jnp.arange(CACHE) < length)[None, None, None, :], cache_scores, -jnp.inf)
        new_scores = jnp.einsum('thgc,uhc->thgu', query_heads, new_keys, precision=precise) * HEAD ** (-0.5)
        causal = jnp.arange(STEPS)[None, :] <= jnp.arange(STEPS)[:, None]
        new_scores = jnp.where(causal[:, None, None, :], new_scores, -jnp.inf)
        highest = jnp.maximum(lax.optimization_barrier(jnp.max(cache_scores, -1)), lax.optimization_barrier(jnp.max(new_scores, -1)))
        cache_weights = jnp.exp(cache_scores - highest[..., None])
        new_weights = jnp.exp(new_scores - highest[..., None])
        denominator = lax.optimization_barrier(jnp.sum(cache_weights, -1)) + lax.optimization_barrier(jnp.sum(new_weights, -1))
        attended = jnp.einsum('thgn,nhc->thgc', cache_weights, cache_values, precision=precise)
        attended = attended + jnp.einsum('thgu,uhc->thgc', new_weights, new_values, precision=precise)
        attended = (attended / denominator[..., None]).reshape(STEPS, QW)
        is_alive = alive_flags[row_index] > 0
        attn_row = jnp.where(is_alive, attended, 0.0).astype(jnp.bfloat16)
        ssm_done = jnp.where(is_alive, ssm_row, 0.0).astype(jnp.bfloat16)
        return (attn_row, ssm_done, carry_state.astype(jnp.bfloat16))
    attn_all, ssm_all, state_all = lax.map(one_row, jnp.arange(ROWS, dtype=jnp.int32))
    return (attn_all, ssm_all, state_all)
```

```python
import functools

import jax
import jax.numpy as jnp
import numpy as np
from jax import lax
from jax.experimental import pallas as pl
from jax.experimental.pallas import tpu as pltpu
from jax.sharding import PartitionSpec as P

HEAD = 128
SSM_HEAD = 64
STATE = 256
KERNEL = 4
STEPS = 4
INNER = 4096
EPSILON = 1e-05
NODE_DEV = 4
GROUP = 5
COLUMNS = 4
MESH = pl.DeviceIdType.MESH
HIGHEST = lax.Precision.HIGHEST

PAIR = 64
BACK = 48
BLOCK = 32


def pair_constants():
    gather = np.zeros((PAIR, 2 * BLOCK), np.float32)
    shift = np.zeros((PAIR, PAIR), np.float32)
    bias = np.full((PAIR, PAIR), -np.inf, np.float32)
    unpack = np.zeros((2, BLOCK, BACK), np.float32)
    for child in range(2):
        for i in range(20):
            gather[child * 20 + i, child * BLOCK + i] = 1
            unpack[child, i, child * 20 + i] = 1
            for u in range(i % 4 + 1):
                bias[child * 20 + i, 48 + child * 4 + u] = 0
        for u in range(4):
            gather[40 + child * 4 + u, child * BLOCK + 20 + u] = 1
            gather[48 + child * 4 + u, child * BLOCK + 24 + u] = 1
            shift[48 + child * 4 + u, 40 + child * 4 + u] = 1
    return gather, shift, bias, unpack


class Slots:
    def __init__(self, ring):
        half = ring // 2
        self.ring, self.half = ring, half
        self.plus_direct, self.plus_transit = {0: 0}, {0: 1}
        self.minus_direct, self.minus_transit = {0: 0}, {}
        self.plus_group, self.minus_group = [(0, 2)], [(0, 1)]
        for k in range(1, half):
            start = 2 + 3 * (k - 1)
            self.plus_direct[k], self.plus_direct[ring - k], self.plus_transit[k] = start, start + 1, start + 2
            self.plus_group.append((start, 3))
            start = 1 + 3 * (k - 1)
            self.minus_direct[k], self.minus_direct[ring - k], self.minus_transit[ring - k] = start, start + 1, start + 2
            self.minus_group.append((start, 3))
        start = 2 + 3 * (half - 1)
        self.plus_direct[half] = start
        self.plus_group.append((start, 1))
        start = 1 + 3 * (half - 1)
        self.minus_direct[half], self.minus_transit[half] = start, start + 1
        self.minus_group.append((start, 2))
        self.sent = 3 * half
        self.plus = ring
        self.minus = ring + self.sent + half
        self.total = ring + 2 * (self.sent + half)

    def table(self):
        place = np.zeros((COLUMNS, self.ring), np.int32)
        for dz in range(self.ring):
            place[0, dz] = dz
            place[3, dz] = self.plus + self.plus_direct[dz]
            place[1, dz] = self.minus + self.minus_direct[dz]
            if dz < self.half:
                place[2, dz] = self.plus + self.sent + dz
            else:
                place[2, dz] = self.minus + self.sent + (self.ring - dz) - 1
        return place.reshape(-1)


def exchange_kernel(
    slots, heads, res_rows,
    tab, pair_rows, len_nodes, len_res, child_src, child_which,
    ssm, conv, comb, kv_nodes, kv_res, gather, shift, bias, unpack,
    arr, carr, att,
    gz, sp, sm, oc, cgz, csp, csm, coc, q_out, q_in, o_out, o_in,
    zsend, zrecv, xsend, xrecv, fsend, frecv, osem,
    czsend, czrecv, cxsend, cxrecv, cfsend, cfrecv, cosem,
    qsend, qrecv, rsend, rrecv,
):
    ring, half = slots.ring, slots.half
    devices = COLUMNS * ring
    me = lax.axis_index("dp")
    tensor = lax.axis_index("tensor")
    x, z = me // ring, me % ring

    def at(column, row):
        return ((column + COLUMNS) % COLUMNS) * ring + (row + ring) % ring

    above, below = at(x, z + 1), at(x, z - 1)
    right, left = at(x + 1, z), at(x - 1, z)
    across = at(x + 2, z)

    barrier = pltpu.get_barrier_semaphore()

    @pl.loop(1, devices)
    def _(step):
        pl.semaphore_signal(
            barrier, inc=1, device_id=((me + step) % devices, tensor), device_id_type=MESH
        )

    pl.semaphore_wait(barrier, devices - 1)

    def send(source, target, send_sem, recv_sem, device):
        return pltpu.make_async_remote_copy(
            src_ref=source,
            dst_ref=target,
            send_sem=send_sem,
            recv_sem=recv_sem,
            device_id=(device, tensor),
            device_id_type=MESH,
        )

    class Stream:
        def __init__(self, own, gz, sp, sm, oc, arr, zsend, zrecv, xsend, xrecv, fsend, frecv, osem):
            self.own, self.gz, self.sp, self.sm, self.oc, self.arr = own, gz, sp, sm, oc, arr
            self.zsend, self.zrecv, self.xsend, self.xrecv = zsend, zrecv, xsend, xrecv
            self.fsend, self.frecv, self.osem = fsend, frecv, osem

        def hop(self, c, k, up):
            if k == 1:
                source = self.own.at[:, c]
            else:
                source = self.gz.at[c, (ring - k + 1 if up else k - 1) - 1]
            target = self.gz.at[c, (ring - k if up else k) - 1]
            if k == half:
                nodes = pl.ds(0 if up else NODE_DEV // 2, NODE_DEV // 2)
                source, target = source.at[nodes], target.at[nodes]
            way = 0 if up else 1
            return send(
                source, target, self.zsend.at[c, way, k - 1], self.zrecv.at[c, way, k - 1],
                above if up else below,
            )

        def across_x(self, c, k, plus):
            start, size = (slots.plus_group if plus else slots.minus_group)[k]
            base = slots.plus if plus else slots.minus
            way = 0 if plus else 1
            return send(
                (self.sp if plus else self.sm).at[c, pl.ds(start, size)],
                self.arr.at[c, pl.ds(base + start, size)],
                self.xsend.at[c, way, k], self.xrecv.at[c, way, k],
                right if plus else left,
            )

        def forward(self, c, k, plus):
            if plus:
                source = slots.plus + slots.plus_transit[k]
                target = slots.plus + slots.sent + k
                index = k
            else:
                source = slots.minus + slots.minus_transit[half if k == half else ring - k]
                target = slots.minus + slots.sent + k - 1
                index = k - 1
            way = 0 if plus else 1
            return send(
                self.arr.at[c, source], self.arr.at[c, target],
                self.fsend.at[c, way, index], self.frecv.at[c, way, index],
                right if plus else left,
            )

        def own_copy(self, c):
            return pltpu.make_async_copy(
                self.oc.at[c], self.arr.at[c, pl.ds(0, ring)], self.osem.at[c]
            )

        def pick(self, c, dz, target):
            node = tab[target * devices + at(x, z + dz)]
            if dz == 0:
                return self.own[node, c]
            picked = self.gz[c, dz - 1, 0]
            for other in range(1, NODE_DEV):
                picked = jnp.where(node == other, self.gz[c, dz - 1, other], picked)
            return picked

        def group(self, c, k):
            rows = [0] if k == 0 else [half] if k == half else [k, ring - k]
            for dz in rows:
                self.sp[c, slots.plus_direct[dz]] = self.pick(c, dz, right)
                self.sm[c, slots.minus_direct[dz]] = self.pick(c, dz, left)
                if dz in slots.plus_transit:
                    self.sp[c, slots.plus_transit[dz]] = self.pick(c, dz, across)
                else:
                    self.sm[c, slots.minus_transit[dz]] = self.pick(c, dz, across)
            self.across_x(c, k, True).start()
            self.across_x(c, k, False).start()
            for dz in rows:
                self.oc[c, dz] = self.pick(c, dz, me)
            if k == half:
                self.own_copy(c).start()

        def stage(self, c, k):
            for up in (True, False):
                if k >= 1:
                    self.hop(c, k, up).wait_recv()
                if k < half:
                    self.hop(c, k + 1, up).start()
            self.group(c, k)

        def relay(self, c, k):
            for plus in (True, False):
                self.across_x(c, k, plus).wait_recv()
                if k in (range(half) if plus else range(1, half + 1)):
                    self.forward(c, k, plus).start()

        def finish(self, c):
            for k in range(1, half + 1):
                for up in (True, False):
                    self.hop(c, k, up).wait_send()
            for k in range(half + 1):
                for plus in (True, False):
                    self.across_x(c, k, plus).wait_send()
                    if k in (range(half) if plus else range(1, half + 1)):
                        self.forward(c, k, plus).wait()
            self.own_copy(c).wait()

    main = Stream(ssm, gz, sp, sm, oc, arr, zsend, zrecv, xsend, xrecv, fsend, frecv, osem)
    side = Stream(
        conv, cgz, csp, csm, coc, carr,
        czsend, czrecv, cxsend, cxrecv, cfsend, cfrecv, cosem,
    )

    def dot(a, b, dims):
        return lax.dot_general(a, b, (dims, ((), ())), preferred_element_type=jnp.float32)

    def weigh(weights, values):
        high = weights.astype(jnp.bfloat16)
        low = (weights - high.astype(jnp.float32)).astype(jnp.bfloat16)
        return dot(high, values, ((1,), (0,))) + dot(low, values, ((1,), (0,)))

    def attend(message, keys, values, length):
        scale = HEAD**-0.5
        old = dot(message, keys, ((1,), (1,))) * scale
        spot = lax.broadcasted_iota(jnp.int32, old.shape, 1)
        old = jnp.where(spot < length, old, -jnp.inf)
        moved = dot(shift[...], message, ((1,), (0,))).astype(jnp.bfloat16)
        new = dot(message, moved, ((1,), (1,))) * scale + bias[...]
        top = jnp.maximum(jnp.max(old, 1, keepdims=True), jnp.max(new, 1, keepdims=True))
        old, new = jnp.exp(old - top), jnp.exp(new - top)
        total = jnp.sum(old, 1, keepdims=True) + jnp.sum(new, 1, keepdims=True)
        return (weigh(old, values) + weigh(new, message)) / total

    def pack(first, second):
        both = jnp.concatenate([comb[first], comb[second]], 0)
        return dot(gather[...], both, ((1,), (0,))).astype(jnp.bfloat16)

    def ask(d):
        return send(q_out.at[d], q_in.at[me], qsend.at[d], qrecv.at[me], d)

    def asked(d):
        return send(q_out.at[d], q_in.at[d], qsend.at[d], qrecv.at[d], d)

    def reply(d):
        return send(o_out.at[d], o_in.at[me], rsend.at[d], rrecv.at[me], d)

    def replied(d):
        return send(o_out.at[d], o_in.at[d], rsend.at[d], rrecv.at[d], d)

    def ask_all():
        @pl.loop(0, devices)
        def _(step):
            d = (me + step) % devices
            message = pack(res_rows + pair_rows[d], res_rows + pair_rows[devices + d])

            @pl.when(step == 0)
            def _():
                q_in[me] = message

            @pl.when(step != 0)
            def _():
                q_out[d] = message
                ask(d).start()

    def serve(step):
        d = (me + devices - step) % devices

        @pl.when(step != 0)
        def _():
            asked(d).wait_recv()

        node = tab[d * devices + me]
        result = attend(q_in[d], kv_nodes[node, 0], kv_nodes[node, 1], len_nodes[me * NODE_DEV + node])
        result = result[:BACK].astype(jnp.bfloat16)

        @pl.when(step == 0)
        def _():
            o_in[me] = result

        @pl.when(step != 0)
        def _():
            o_out[d] = result
            reply(d).start()

    def resident(row):
        result = attend(pack(row, row), kv_res[row, 0], kv_res[row, 1], len_res[row])
        att[row] = result[:BLOCK].astype(jnp.bfloat16)

    batch = 4
    begin = [0] + [k + 1 for k in range(1, half + 1)]

    @pl.loop(0, heads + half + 2)
    def _(tick):
        for k in range(half, -1, -1):
            c = tick - begin[k]

            @pl.when(c == 0)
            def _():
                side.stage(0, k)

            @pl.when((c >= 0) & (c < heads))
            def _():
                main.stage(c, k)

        for k in range(half, -1, -1):
            c = tick - begin[k] - 1

            @pl.when(c == 0)
            def _():
                side.relay(0, k)

            @pl.when((c >= 0) & (c < heads))
            def _():
                main.relay(c, k)

        @pl.when(tick == 0)
        def _():
            ask_all()

        @pl.when(tick == 1)
        def _():
            @pl.loop(0, res_rows)
            def _(row):
                resident(row)

        @pl.when((tick >= 2) & (tick < 2 + devices // batch))
        def _():
            @pl.loop(0, batch)
            def _(i):
                serve((tick - 2) * batch + i)

    @pl.loop(1, devices)
    def _(step):
        d = (me + step) % devices
        replied(d).wait_recv()

    @pl.loop(0, child_src.shape[0])
    def _(child):
        mine = jnp.where(child_which[child] == 1, unpack[1], unpack[0])
        att[res_rows + child] = dot(mine, o_in[child_src[child]], ((1,), (0,))).astype(jnp.bfloat16)

    side.finish(0)

    @pl.loop(0, heads)
    def _(c):
        main.finish(c)

    @pl.loop(1, devices)
    def _(step):
        d = (me + step) % devices
        ask(d).wait_send()
        reply(d).wait_send()


def exchange(tab, pair_rows, len_nodes, len_res, child_src, child_which, ssm, conv, comb, kv_nodes, kv_res, ring):
    slots = Slots(ring)
    half = ring // 2
    devices = COLUMNS * ring
    heads = ssm.shape[1]
    rows = comb.shape[0]
    gather, shift, bias, unpack = pair_constants()
    smem = pl.BlockSpec(memory_space=pltpu.SMEM)
    vmem = pl.BlockSpec(memory_space=pltpu.VMEM)
    anywhere = pl.BlockSpec(memory_space=pl.ANY)
    bf16 = jnp.bfloat16

    def buffers(count, height):
        return [
            pltpu.VMEM((count, ring - 1, NODE_DEV, height, STATE), bf16),
            pltpu.VMEM((count, slots.sent, height, STATE), bf16),
            pltpu.VMEM((count, slots.sent, height, STATE), bf16),
            pltpu.VMEM((count, ring, height, STATE), bf16),
        ]

    def semaphores(count):
        dma = pltpu.SemaphoreType.DMA
        return [
            dma((count, 2, half)), dma((count, 2, half)),
            dma((count, 2, half + 1)), dma((count, 2, half + 1)),
            dma((count, 2, half)), dma((count, 2, half)),
            dma((count,)),
        ]

    return pl.pallas_call(
        functools.partial(exchange_kernel, slots, heads, kv_res.shape[0]),
        out_shape=[
            jax.ShapeDtypeStruct((heads, slots.total, SSM_HEAD, STATE), bf16),
            jax.ShapeDtypeStruct((1, slots.total, 16, STATE), bf16),
            jax.ShapeDtypeStruct((rows, BLOCK, HEAD), bf16),
        ],
        in_specs=[smem] * 6 + [vmem] * 9,
        out_specs=[anywhere, anywhere, vmem],
        scratch_shapes=buffers(heads, SSM_HEAD)
        + buffers(1, 16)
        + [
            pltpu.VMEM((devices, PAIR, HEAD), bf16),
            pltpu.VMEM((devices, PAIR, HEAD), bf16),
            pltpu.VMEM((devices, BACK, HEAD), bf16),
            pltpu.VMEM((devices, BACK, HEAD), bf16),
        ]
        + semaphores(heads)
        + semaphores(1)
        + [pltpu.SemaphoreType.DMA((devices,))] * 4,
        compiler_params=pltpu.CompilerParams(
            collective_id=0, has_side_effects=True, vmem_limit_bytes=40 * 1024 * 1024
        ),
        name="exchange",
    )(
        tab, pair_rows, len_nodes, len_res, child_src, child_which,
        ssm, conv, comb, kv_nodes, kv_res,
        jnp.asarray(gather, bf16), jnp.asarray(shift, bf16), jnp.asarray(bias), jnp.asarray(unpack, bf16),
    )


def state_kernel(res_rows, place, last_decay, res, arr, c_parts, b_parts, w_parts, new_ssm, read):
    row = pl.program_id(0)
    heads = res.shape[1]

    def work(state):
        sums = lax.dot_general(
            c_parts[0], state, (((1,), (1,)), ((), ())), preferred_element_type=jnp.float32
        )
        read[0] = sums[0:4] + sums[4:8] + sums[8:12]
        added = lax.dot_general(
            w_parts[0], b_parts[0], (((0,), (0,)), ((), ())), preferred_element_type=jnp.float32
        )
        for h in range(heads):
            span = slice(h * SSM_HEAD, (h + 1) * SSM_HEAD)
            new = last_decay[row * heads + h] * state[span].astype(jnp.float32) + added[span]
            new_ssm[0, h] = new.astype(jnp.bfloat16)

    @pl.when(row < res_rows)
    def _():
        work(res[0].reshape(heads * SSM_HEAD, STATE))

    @pl.when(row >= res_rows)
    def _():
        work(arr[:, 0].reshape(heads * SSM_HEAD, STATE))


def update_states(place, last_decay, res, arr, c_parts, b_parts, w_parts):
    res_rows, heads = res.shape[:2]
    rows = c_parts.shape[0]
    features = heads * SSM_HEAD

    def by_row(shape):
        return pl.BlockSpec((1,) + shape, lambda r, p, d: (r,) + (0,) * len(shape))

    return pl.pallas_call(
        functools.partial(state_kernel, res_rows),
        out_shape=[
            jax.ShapeDtypeStruct((rows, heads, SSM_HEAD, STATE), jnp.bfloat16),
            jax.ShapeDtypeStruct((rows, STEPS, features), jnp.float32),
        ],
        grid_spec=pltpu.PrefetchScalarGridSpec(
            num_scalar_prefetch=2,
            grid=(rows,),
            in_specs=[
                pl.BlockSpec(
                    (1, heads, SSM_HEAD, STATE), lambda r, p, d: (jnp.minimum(r, res_rows - 1), 0, 0, 0)
                ),
                pl.BlockSpec((heads, 1, SSM_HEAD, STATE), lambda r, p, d: (0, p[r], 0, 0)),
                by_row((16, STATE)),
                by_row((16, STATE)),
                by_row((16, features)),
            ],
            out_specs=[by_row((heads, SSM_HEAD, STATE)), by_row((STEPS, features))],
        ),
        name="states",
    )(place, last_decay, res, arr, c_parts, b_parts, w_parts)


def norm_kernel(peers, read, decay, rest, gate, gain, alive, out, sums, landed, send_sem, recv_sem):
    me = lax.axis_index("tensor")
    dp = lax.axis_index("dp")
    if peers > 1:
        barrier = pltpu.get_barrier_semaphore()

        @pl.loop(1, peers)
        def _(step):
            pl.semaphore_signal(
                barrier, inc=1, device_id=(dp, (me + step) % peers), device_id_type=MESH
            )

    gated = (read[...] * decay[...] + rest[...]) * jax.nn.silu(gate[...].astype(jnp.float32))
    total = lax.dot_general(
        jnp.ones((8, gated.shape[1]), jnp.float32), gated * gated, (((1,), (1,)), ((), ())),
        precision=HIGHEST, preferred_element_type=jnp.float32,
    )
    sums[...] = total

    def copy(d, slot):
        return pltpu.make_async_remote_copy(
            src_ref=sums, dst_ref=landed.at[slot], send_sem=send_sem.at[d], recv_sem=recv_sem.at[slot],
            device_id=(dp, d), device_id_type=MESH,
        )

    if peers > 1:
        pl.semaphore_wait(barrier, peers - 1)

        @pl.loop(1, peers)
        def _(step):
            copy((me + step) % peers, me).start()

        @pl.loop(1, peers)
        def _(step):
            d = (me + step) % peers
            copy(d, d).wait_recv()

        landed[me] = sums[...]
        total = landed[0]
        for d in range(1, peers):
            total = total + landed[d]
    scale = lax.rsqrt(total / INNER + EPSILON)
    first = lax.broadcasted_iota(jnp.int32, scale.shape, 0) == 0
    column = lax.dot_general(
        jnp.where(first, scale, 0.0), jnp.ones((8, 128), jnp.float32), (((0,), (0,)), ((), ())),
        precision=HIGHEST, preferred_element_type=jnp.float32,
    )
    result = gated * column[:, 0:1] * gain[...]
    out[...] = jnp.where(alive[...] > 0, result, 0.0).astype(jnp.bfloat16)
    if peers > 1:

        @pl.loop(1, peers)
        def _(step):
            copy((me + step) % peers, me).wait_send()


def gated_norm(read, decay, rest, gate, gain, alive, peers):
    lines, features = read.shape
    return pl.pallas_call(
        functools.partial(norm_kernel, peers),
        out_shape=jax.ShapeDtypeStruct((lines, features), jnp.bfloat16),
        in_specs=[pl.BlockSpec(memory_space=pltpu.VMEM)] * 6,
        out_specs=pl.BlockSpec(memory_space=pltpu.VMEM),
        scratch_shapes=[
            pltpu.VMEM((8, lines), jnp.float32),
            pltpu.VMEM((peers, 8, lines), jnp.float32),
            pltpu.SemaphoreType.DMA((peers,)),
            pltpu.SemaphoreType.DMA((peers,)),
        ],
        compiler_params=pltpu.CompilerParams(collective_id=1 if peers > 1 else None, has_side_effects=True),
        name="norm",
    )(read, decay, rest, gate, gain, alive)


def split(value, parts):
    pieces = []
    for _ in range(parts):
        piece = lax.reduce_precision(value, 8, 7)
        pieces.append(piece.astype(jnp.bfloat16))
        value = value - piece
    return pieces


def per_device(
    ssm_resident, ssm_nodes, conv_resident, conv_nodes, convbc_resident, convbc_nodes,
    kv_resident, kv_nodes, len_resident, len_nodes, parents, alive_flags, queries, new_kv,
    x_in, gate_in, bc_in, dt_in, conv_x_weight, conv_bc_weight, a_log, dt_bias, skip_gain, norm_gain,
):
    devices = lax.axis_size("dp")
    peers = lax.axis_size("tensor")
    me = lax.axis_index("dp")
    ring = devices // COLUMNS
    child_dev = parents.shape[0] // devices
    rows = queries.shape[0]
    res_rows = ssm_resident.shape[0]
    heads = ssm_nodes.shape[1]
    features = heads * SSM_HEAD
    bf16, f32 = jnp.bfloat16, jnp.float32

    grouped = parents.reshape(devices, child_dev)
    match = (grouped // NODE_DEV)[:, None, :] == jnp.arange(devices)[None, :, None]
    tab = jnp.max(jnp.where(match, (grouped % NODE_DEV)[:, None, :], 0), axis=2).reshape(-1)
    own = lax.dynamic_slice_in_dim(parents, me * child_dev, child_dev)
    child_src = own // NODE_DEV
    mine = child_src[None, :] == jnp.arange(devices)[:, None]
    number = jnp.arange(child_dev)[None, :]
    first = jnp.min(jnp.where(mine, number, child_dev - 1), axis=1)
    second = jnp.max(jnp.where(mine, number, 0), axis=1)
    child_which = jnp.sum(jnp.where(mine & (number > first[:, None]), 1, 0), axis=0)
    relative = (
        (child_src // ring - me // ring) % COLUMNS * ring + (child_src % ring - me % ring) % ring
    )
    place = jnp.take(jnp.asarray(Slots(ring).table()), relative)

    convs = conv_nodes.reshape(NODE_DEV, -1, STATE)
    convbcs = convbc_nodes.reshape(NODE_DEV, -1, STATE)
    used = convs.shape[1]
    convp = jnp.concatenate(
        [convs, convbcs, jnp.zeros((NODE_DEV, 16 - used - 6, STATE), bf16)], 1
    )[:, None]
    comb = jnp.concatenate(
        [
            queries.reshape(rows, STEPS, GROUP, HEAD).transpose(0, 2, 1, 3).reshape(rows, 20, HEAD),
            new_kv.reshape(rows, 2 * STEPS, HEAD),
            jnp.zeros((rows, 4, HEAD), bf16),
        ],
        1,
    )
    arr, carr, att = exchange(
        tab, jnp.concatenate([first, second]), len_nodes, len_resident, child_src, child_which,
        ssm_nodes, convp, comb, kv_nodes, kv_resident, ring,
    )

    got = jnp.take(carr[0], place, axis=0)
    all_conv = jnp.concatenate([conv_resident, got[:, :used].reshape(child_dev, KERNEL - 1, -1)], 0)
    all_convbc = jnp.concatenate(
        [convbc_resident, got[:, used : used + 6].reshape(child_dev, KERNEL - 1, -1)], 0
    )
    conv_input = jnp.concatenate([all_conv, x_in], 1).astype(f32)
    conv_bc_input = jnp.concatenate([all_convbc, bc_in], 1).astype(f32)
    mixed_x = jnp.zeros(x_in.shape, f32)
    mixed_bc = jnp.zeros(bc_in.shape, f32)
    for tap in range(KERNEL):
        mixed_x = mixed_x + conv_x_weight[tap].astype(f32) * conv_input[:, tap : tap + STEPS]
        mixed_bc = mixed_bc + conv_bc_weight[tap].astype(f32) * conv_bc_input[:, tap : tap + STEPS]
    mixed_x = jax.nn.silu(mixed_x)
    mixed_bc = jax.nn.silu(mixed_bc)
    b_part = mixed_bc[:, :, :STATE]
    c_part = mixed_bc[:, :, STATE:]
    dt = jax.nn.softplus(dt_in.astype(f32) + dt_bias)
    decay = jnp.exp(-jnp.exp(a_log) * dt)

    def spread(value):
        return jnp.repeat(value, SSM_HEAD, axis=-1)

    rest, since = [], []
    scaled = [spread(dt[:, t]) * mixed_x[:, t] for t in range(STEPS)]
    carried = []
    for t in range(STEPS):
        step_decay = decay[:, t]
        since = [d * step_decay for d in since] + [jnp.ones_like(step_decay)]
        carried.append(step_decay if t == 0 else carried[-1] * step_decay)
        value = spread(skip_gain) * mixed_x[:, t]
        for s in range(t + 1):
            overlap = jnp.sum(c_part[:, t] * b_part[:, s], -1, keepdims=True)
            value = value + spread(since[s]) * overlap * scaled[s]
        rest.append(value)
    rest = jnp.stack(rest, 1)
    carried = jnp.stack(carried, 1)
    weights = jnp.stack([spread(since[s]) * scaled[s] for s in range(STEPS)], 1)

    def padded(pieces):
        return jnp.concatenate(pieces + [jnp.zeros_like(pieces[0])], 1)

    c_parts = padded(split(c_part, 3))
    b_high, b_low = split(b_part, 2)
    w_high, w_low = split(weights, 2)
    b_parts = padded([b_high, b_low, b_high])
    w_parts = padded([w_high, w_high, w_low])
    place_all = jnp.concatenate([jnp.broadcast_to(place[0], (res_rows,)), place])
    new_ssm, read = update_states(
        place_all, carried[:, -1].reshape(-1), ssm_resident, arr, c_parts, b_parts, w_parts
    )
    lines = rows * STEPS
    alive = jnp.repeat(alive_flags, STEPS)[:, None]
    ssm_out = gated_norm(
        read.reshape(lines, features),
        spread(carried).reshape(lines, features),
        rest.reshape(lines, features),
        gate_in.reshape(lines, features),
        norm_gain[None, :],
        alive,
        peers,
    ).reshape(rows, STEPS, features)
    attn = att[:, :20].reshape(rows, GROUP, STEPS, HEAD).transpose(0, 2, 1, 3).reshape(rows, STEPS, -1)
    attn = jnp.where((alive_flags > 0)[:, None, None], attn, jnp.zeros((), bf16))
    return attn, ssm_out, new_ssm


def solution(mesh):
    return jax.shard_map(
        per_device,
        mesh=mesh,
        in_specs=(
            P("dp", "tensor", None, None),
            P("dp", "tensor", None, None),
            P("dp", None, "tensor"),
            P("dp", None, "tensor"),
            P("dp", None, None),
            P("dp", None, None),
            P("dp", None, None, "tensor"),
            P("dp", None, None, "tensor"),
            P("dp"),
            P(),
            P(),
            P("dp"),
            P("dp", None, "tensor"),
            P("dp", None, None, "tensor"),
            P("dp", None, "tensor"),
            P("dp", None, "tensor"),
            P("dp", None, None),
            P("dp", None, "tensor"),
            P(None, "tensor"),
            P(),
            P("tensor"),
            P("tensor"),
            P("tensor"),
            P("tensor"),
        ),
        out_specs=(P("dp", None, "tensor"), P("dp", None, "tensor"), P("dp", "tensor", None, None)),
        check_vma=False,
    )
```

```python
import functools

import jax
import jax.numpy as jnp
import numpy as np
from jax import lax
from jax.experimental import pallas as pl
from jax.experimental.pallas import tpu as pltpu
from jax.sharding import PartitionSpec as P

HEAD = 128
SSM_HEAD = 64
STATE = 256
KERNEL = 4
STEPS = 4
INNER = 4096
EPSILON = 1e-05
NODE_DEV = 4
GROUP = 5
COLUMNS = 4
MESH = pl.DeviceIdType.MESH


class Slots:
    def __init__(self, ring):
        half = ring // 2
        self.ring, self.half = ring, half
        self.plus_direct, self.plus_transit = {0: 0}, {0: 1}
        self.minus_direct, self.minus_transit = {0: 0}, {}
        self.plus_group, self.minus_group = [(0, 2)], [(0, 1)]
        for k in range(1, half):
            start = 2 + 3 * (k - 1)
            self.plus_direct[k], self.plus_direct[ring - k], self.plus_transit[k] = start, start + 1, start + 2
            self.plus_group.append((start, 3))
            start = 1 + 3 * (k - 1)
            self.minus_direct[k], self.minus_direct[ring - k], self.minus_transit[ring - k] = start, start + 1, start + 2
            self.minus_group.append((start, 3))
        start = 2 + 3 * (half - 1)
        self.plus_direct[half] = start
        self.plus_group.append((start, 1))
        start = 1 + 3 * (half - 1)
        self.minus_direct[half], self.minus_transit[half] = start, start + 1
        self.minus_group.append((start, 2))
        self.sent = 3 * half
        self.plus = ring
        self.minus = ring + self.sent + half
        self.total = ring + 2 * (self.sent + half)

    def table(self):
        place = np.zeros((COLUMNS, self.ring), np.int32)
        for dz in range(self.ring):
            place[0, dz] = dz
            place[3, dz] = self.plus + self.plus_direct[dz]
            place[1, dz] = self.minus + self.minus_direct[dz]
            if dz < self.half:
                place[2, dz] = self.plus + self.sent + dz
            else:
                place[2, dz] = self.minus + self.sent + (self.ring - dz) - 1
        return place.reshape(-1)


PAIR = 64
BACK = 48
BLOCK = 32
GROUPS = 2


def dot(a, b, dims):
    return lax.dot_general(a, b, (dims, ((), ())), preferred_element_type=jnp.float32)


def silu(value):
    return value / (1.0 + jnp.exp(-value))


def softplus(value):
    return jnp.maximum(value, 0.0) + jnp.log1p(jnp.exp(-jnp.abs(value)))


def split(value, parts):
    pieces = []
    for _ in range(parts):
        piece = value.astype(jnp.bfloat16).astype(jnp.float32)
        pieces.append(piece)
        value = value - piece
    return pieces


def round_kernel(
    slots, heads, res_rows, child_dev, peers,
    plan, len_nodes, len_res, alive, a_log, dt_bias, skip_gain,
    ssm_h, res_h, kvn_h, kvr_h, q_h, nkv_h, x_h, g_h, bc_h, dt_h, cr_h, cbr_h, cn_h, cbn_h, wx_h, wbc_h, gain_h,
    att, ssm_out, new_out,
    *scratch,
):
    scratch = list(scratch)

    def take(count):
        taken, scratch[:count] = scratch[:count], []
        return taken

    loaded = take(17)
    (ssm, res, kv_nodes, kv_res, q_v, nkv_v, x_v, g_v, bc_v, dt_v, cr_v, cbr_v, cn_v, cbn_v, wx_v, wbc_v, gain_v) = loaded
    (load_sem,) = take(1)
    comb, convp, new_v, gather, shift, bias = take(6)
    ux, ub, c_parts, b_parts, w_parts, carried, rest, read = take(8)
    q_out, q_in, o_out, o_in = take(4)
    qsend, qrecv, rsend, rrecv = take(4)
    sums, landed, psend, precv = take(4)
    (new_sem,) = take(1)

    ring, half = slots.ring, slots.half
    devices = COLUMNS * ring
    rows = res_rows + child_dev
    features = heads * SSM_HEAD
    me = lax.axis_index("dp")
    tensor = lax.axis_index("tensor")
    x, z = me // ring, me % ring
    first_at = devices * devices
    second_at = first_at + devices
    src_at = second_at + devices
    which_at = src_at + child_dev
    place_at = which_at + child_dev

    sources = (ssm_h, res_h, kvn_h, kvr_h, q_h, nkv_h, x_h, g_h, bc_h, dt_h, cr_h, cbr_h, cn_h, cbn_h, wx_h, wbc_h, gain_h)
    loads = [pltpu.make_async_copy(a, b, load_sem.at[i]) for i, (a, b) in enumerate(zip(sources, loaded))]
    for load in loads:
        load.start()

    barrier = pltpu.get_barrier_semaphore()

    @pl.loop(1, devices)
    def _(step):
        pl.semaphore_signal(
            barrier, inc=1, device_id=((me + step) % devices, tensor), device_id_type=MESH
        )

    if peers > 1:

        @pl.loop(1, peers)
        def _(step):
            pl.semaphore_signal(
                barrier, inc=1, device_id=(me, (tensor + step) % peers), device_id_type=MESH
            )

    for load in loads:
        load.wait()

    def at(column, row):
        return ((column + COLUMNS) % COLUMNS) * ring + (row + ring) % ring

    above, below = at(x, z + 1), at(x, z - 1)
    right, left = at(x + 1, z), at(x - 1, z)
    across = at(x + 2, z)

    for node in range(NODE_DEV):
        lines = []
        for value in (cn_v, cbn_v):
            for j in range(KERNEL - 1):
                for begin in range(0, value.shape[2], STATE):
                    lines.append(value[j].astype(jnp.float32)[node : node + 1, begin : begin + STATE])
        used = len(lines)
        lines.append(jnp.zeros((16 - used, STATE), jnp.float32))
        convp[node, 0] = jnp.concatenate(lines, 0).astype(jnp.bfloat16)
    x_lines = (KERNEL - 1) * features // STATE

    pl.semaphore_wait(barrier, devices - 1 + peers - 1)

    def send(source, target, send_sem, recv_sem, device):
        return pltpu.make_async_remote_copy(
            src_ref=source,
            dst_ref=target,
            send_sem=send_sem,
            recv_sem=recv_sem,
            device_id=(device, tensor),
            device_id_type=MESH,
        )

    class Stream:
        def __init__(self, own, base, refs):
            self.own, self.base = own, base
            (self.gz, self.sp, self.sm, self.arr,
             self.zsend, self.zrecv, self.xsend, self.xrecv, self.fsend, self.frecv) = refs

        def hop(self, c, k, up):
            if k == 1:
                source = self.own.at[:, self.base + c]
            else:
                source = self.gz.at[c, (ring - k + 1 if up else k - 1) - 1]
            target = self.gz.at[c, (ring - k if up else k) - 1]
            if k == half:
                nodes = pl.ds(0 if up else NODE_DEV // 2, NODE_DEV // 2)
                source, target = source.at[nodes], target.at[nodes]
            way = 0 if up else 1
            return send(
                source, target, self.zsend.at[c, way, k - 1], self.zrecv.at[c, way, k - 1],
                above if up else below,
            )

        def across_x(self, c, k, plus):
            start, size = (slots.plus_group if plus else slots.minus_group)[k]
            base = slots.plus if plus else slots.minus
            way = 0 if plus else 1
            return send(
                (self.sp if plus else self.sm).at[c, pl.ds(start, size)],
                self.arr.at[c, pl.ds(base + start, size)],
                self.xsend.at[c, way, k], self.xrecv.at[c, way, k],
                right if plus else left,
            )

        def forward(self, c, k, plus):
            if plus:
                source = slots.plus + slots.plus_transit[k]
                target = slots.plus + slots.sent + k
                index = k
            else:
                source = slots.minus + slots.minus_transit[half if k == half else ring - k]
                target = slots.minus + slots.sent + k - 1
                index = k - 1
            way = 0 if plus else 1
            return send(
                self.arr.at[c, source], self.arr.at[c, target],
                self.fsend.at[c, way, index], self.frecv.at[c, way, index],
                right if plus else left,
            )

        def pick(self, c, dz, target):
            node = plan[target * devices + at(x, z + dz)]
            if dz == 0:
                return self.own[node, self.base + c]
            picked = self.gz[c, dz - 1, 0]
            for other in range(1, NODE_DEV):
                picked = jnp.where(node == other, self.gz[c, dz - 1, other], picked)
            return picked

        def group(self, c, k):
            dzs = [0] if k == 0 else [half] if k == half else [k, ring - k]
            for dz in dzs:
                self.sp[c, slots.plus_direct[dz]] = self.pick(c, dz, right)
                self.sm[c, slots.minus_direct[dz]] = self.pick(c, dz, left)
                if dz in slots.plus_transit:
                    self.sp[c, slots.plus_transit[dz]] = self.pick(c, dz, across)
                else:
                    self.sm[c, slots.minus_transit[dz]] = self.pick(c, dz, across)
            self.across_x(c, k, True).start()
            self.across_x(c, k, False).start()
            for dz in dzs:
                self.arr[c, dz] = self.pick(c, dz, me)

        def stage(self, c, k):
            for up in (True, False):
                if k >= 1:
                    self.hop(c, k, up).wait_recv()
                if k < half:
                    self.hop(c, k + 1, up).start()
            self.group(c, k)

        def relay(self, c, k):
            for plus in (True, False):
                self.across_x(c, k, plus).wait_recv()
                if k in (range(half) if plus else range(1, half + 1)):
                    self.forward(c, k, plus).start()

        def arrive(self, c):
            for k in range(half + 1):
                for plus in (True, False):
                    if k in (range(half) if plus else range(1, half + 1)):
                        self.forward(c, k, plus).wait_recv()

        def finish(self, c):
            for k in range(1, half + 1):
                for up in (True, False):
                    self.hop(c, k, up).wait_send()
            for k in range(half + 1):
                for plus in (True, False):
                    self.across_x(c, k, plus).wait_send()
                    if k in (range(half) if plus else range(1, half + 1)):
                        self.forward(c, k, plus).wait_send()

    per_group = heads // GROUPS
    main = [Stream(ssm, i * per_group, take(10)) for i in range(GROUPS)]
    side = Stream(convp, 0, take(10))

    def on_head(tick, offset, act):
        c = tick - offset
        for i in range(GROUPS):

            @pl.when((c >= i * per_group) & (c < (i + 1) * per_group))
            def _():
                act(main[i], c - i * per_group)

    def weigh(weights, values):
        high = weights.astype(jnp.bfloat16)
        low = (weights - high.astype(jnp.float32)).astype(jnp.bfloat16)
        return dot(high, values, ((1,), (0,))) + dot(low, values, ((1,), (0,)))

    def attend(message, keys, values, length):
        scale = HEAD**-0.5
        old = dot(message, keys, ((1,), (1,))) * scale
        spot = lax.broadcasted_iota(jnp.int32, old.shape, 1)
        old = jnp.where(spot < length, old, -jnp.inf)
        moved = dot(shift[...], message, ((1,), (0,))).astype(jnp.bfloat16)
        new = dot(message, moved, ((1,), (1,))) * scale + bias[...]
        top = jnp.maximum(jnp.max(old, 1, keepdims=True), jnp.max(new, 1, keepdims=True))
        old, new = jnp.exp(old - top), jnp.exp(new - top)
        total = jnp.sum(old, 1, keepdims=True) + jnp.sum(new, 1, keepdims=True)
        return (weigh(old, values) + weigh(new, message)) / total

    def pack(first, second):
        both = jnp.concatenate([comb[first], comb[second]], 0)
        return dot(gather[...], both, ((1,), (0,))).astype(jnp.bfloat16)

    def ask(d):
        return send(q_out.at[d], q_in.at[me], qsend.at[d], qrecv.at[me], d)

    def asked(d):
        return send(q_out.at[d], q_in.at[d], qsend.at[d], qrecv.at[d], d)

    def reply(d):
        return send(o_out.at[d], o_in.at[me], rsend.at[d], rrecv.at[me], d)

    def replied(d):
        return send(o_out.at[d], o_in.at[d], rsend.at[d], rrecv.at[d], d)

    def prepare():
        r = lax.broadcasted_iota(jnp.int32, (PAIR, PAIR), 0)
        c = lax.broadcasted_iota(jnp.int32, (PAIR, PAIR), 1)
        query = r + jnp.where(r >= 20, 12, 0)
        key = r - 20 + jnp.where(r >= 44, 28, 0)
        value = r - 24 + jnp.where(r >= 52, 28, 0)
        column = jnp.where(r < 40, query, jnp.where(r < 48, key, jnp.where(r < 56, value, -1)))
        gather[...] = jnp.where(column == c, 1.0, 0.0).astype(jnp.bfloat16)
        shift[...] = jnp.where((r >= 48) & (r < 56) & (c == r - 8), 1.0, 0.0).astype(jnp.bfloat16)
        same = jnp.where(c >= 52, 1, 0) == jnp.where(r >= 20, 1, 0)
        seen = (r < 40) & (c >= 48) & (c < 56) & same & ((c & 3) <= (r & 3))
        bias[...] = jnp.where(seen, 0.0, -jnp.inf)

        @pl.loop(0, rows)
        def _(row):
            query = q_v[row].astype(jnp.float32)
            lines = [query[:, g * HEAD : (g + 1) * HEAD] for g in range(GROUP)]
            fresh = nkv_v[row].astype(jnp.float32)
            lines += [fresh[0], fresh[1], jnp.zeros((4, HEAD), jnp.float32)]
            comb[row] = jnp.concatenate(lines, 0).astype(jnp.bfloat16)

    def ask_all():
        @pl.loop(0, devices)
        def _(step):
            d = (me + step) % devices
            message = pack(res_rows + plan[first_at + d], res_rows + plan[second_at + d])

            @pl.when(step == 0)
            def _():
                q_in[me] = message

            @pl.when(step != 0)
            def _():
                q_out[d] = message
                ask(d).start()

    def serve(step):
        d = (me + devices - step) % devices

        @pl.when(step != 0)
        def _():
            asked(d).wait_recv()

        node = plan[d * devices + me]
        result = attend(q_in[d], kv_nodes[node, 0], kv_nodes[node, 1], len_nodes[me * NODE_DEV + node])
        result = result[:BACK].astype(jnp.bfloat16)

        @pl.when(step == 0)
        def _():
            o_in[me] = result

        @pl.when(step != 0)
        def _():
            o_out[d] = result
            reply(d).start()

    def put_attended(row, value):
        value = jnp.where(alive[row] > 0, value, 0.0).astype(jnp.bfloat16)
        for g in range(GROUP):
            att[row, :, g * HEAD : (g + 1) * HEAD] = value[4 * g : 4 * g + 4]

    def resident(row):
        put_attended(row, attend(pack(row, row), kv_res[row, 0], kv_res[row, 1], len_res[row])[:20])

    def convolve():
        for j in range(KERNEL - 1):
            ux[j, 0:res_rows] = cr_v[j].astype(jnp.float32)
            ub[j, 0:res_rows] = cbr_v[j].astype(jnp.float32)
        carr = side.arr
        for child in range(child_dev):
            lines = carr[0, plan[place_at + child]].astype(jnp.float32)
            at_row = slice(res_rows + child, res_rows + child + 1)
            line = 0
            for target in (ux, ub):
                for j in range(KERNEL - 1):
                    for begin in range(0, target.shape[2], STATE):
                        target[j, at_row, begin : begin + STATE] = lines[line : line + 1]
                        line += 1
        fresh_x = x_v[...].astype(jnp.float32)
        fresh_b = bc_v[...].astype(jnp.float32)
        for t in range(STEPS):
            ux[KERNEL - 1 + t] = fresh_x[:, t, :]
            ub[KERNEL - 1 + t] = fresh_b[:, t, :]
        weights_x = wx_v[...].astype(jnp.float32)
        weights_b = wbc_v[...].astype(jnp.float32)

        def mix(source, weights, t):
            total = weights[0:1] * source[t]
            for tap in range(1, KERNEL):
                total = total + weights[tap : tap + 1] * source[t + tap]
            return silu(total)

        lane = lax.broadcasted_iota(jnp.int32, (1, features), 1)

        def spread(table):
            value = jnp.zeros((1, features), jnp.float32)
            for h in range(heads):
                inside = (lane >= h * SSM_HEAD) & (lane < (h + 1) * SSM_HEAD)
                value = jnp.where(inside, table[h], value)
            return value

        rate, offset, skip = -jnp.exp(spread(a_log)), spread(dt_bias), spread(skip_gain)
        head = lax.broadcasted_iota(jnp.int32, (heads, features), 0) * SSM_HEAD
        lanes = lax.broadcasted_iota(jnp.int32, (heads, features), 1)
        one_hot = jnp.where((lanes >= head) & (lanes < head + SSM_HEAD), 1.0, 0.0).astype(jnp.bfloat16)
        b_list = []
        c_parts[...] = jnp.zeros(c_parts.shape, jnp.float32)
        b_parts[...] = jnp.zeros(b_parts.shape, jnp.float32)
        w_parts[...] = jnp.zeros(w_parts.shape, jnp.float32)
        since = []
        for t in range(STEPS):
            both = mix(ub, weights_b, t)
            b, c = both[:, :STATE], both[:, STATE:]
            b_list.append(b)
            for part, piece in enumerate(split(c, 3)):
                c_parts[part * 4 + t] = piece
            high, low = split(b, 2)
            b_parts[t], b_parts[4 + t], b_parts[8 + t] = high, low, high
            dt = softplus(dot(dt_v[t], one_hot, ((0,), (0,))) + offset)
            decay = jnp.exp(rate * dt)
            mixed = mix(ux, weights_x, t)
            carried[t] = decay if t == 0 else carried[t - 1] * decay
            since = [value * decay for value in since] + [dt * mixed]
            total = skip * mixed
            for s in range(t + 1):
                total = total + since[s] * jnp.sum(c * b_list[s], 1, keepdims=True)
            rest[t] = total
        for s in range(STEPS):
            high, low = split(since[s], 2)
            w_parts[s], w_parts[4 + s], w_parts[8 + s] = high, high, low

    def new_copy(row, i):
        span = pl.ds(i * per_group, per_group)
        return pltpu.make_async_copy(new_v.at[row, span], new_out.at[row, span], new_sem.at[row, i])

    def update(row, i, state):
        span = slice(i * per_group * SSM_HEAD, (i + 1) * per_group * SSM_HEAD)
        width = per_group * SSM_HEAD
        here = pl.ds(row, 1)
        state = state.reshape(width, STATE)
        c_row = c_parts[:, here, :].reshape(16, STATE).astype(jnp.bfloat16)
        b_row = b_parts[:, here, :].reshape(16, STATE).astype(jnp.bfloat16)
        w_row = w_parts[:, here, span].reshape(16, width).astype(jnp.bfloat16)
        got = dot(c_row, state, ((1,), (1,)))
        read[:, here, span] = (got[0:4] + got[4:8] + got[8:12]).reshape(STEPS, 1, width)
        added = dot(w_row, b_row, ((0,), (0,)))
        last = carried[STEPS - 1, here, span]
        for h in range(per_group):
            part = slice(h * SSM_HEAD, (h + 1) * SSM_HEAD)
            factor = last[:, h * SSM_HEAD : h * SSM_HEAD + 1]
            new = factor * state[part].astype(jnp.float32) + added[part]
            new_v[row, i * per_group + h] = new.astype(jnp.bfloat16)
        new_copy(row, i).start()

    def update_resident(row):
        for i in range(GROUPS):
            update(row, i, res[row, i * per_group : (i + 1) * per_group])

    def update_child(child, i):
        update(res_rows + child, i, main[i].arr[:, plan[place_at + child]])

    batch = 4
    begin = [2 * k for k in range(half + 1)]
    ticks = heads + begin[half] + 1
    ready = begin[half] + 2
    landed_at = per_group + begin[half] + 1
    share = -(-child_dev // (ticks - landed_at))

    @pl.loop(0, ticks)
    def _(tick):
        for k in range(half, -1, -1):

            @pl.when(tick == begin[k])
            def _():
                side.stage(0, k)

            on_head(tick, begin[k], lambda stream, c: stream.stage(c, k))
        for k in range(half, -1, -1):

            @pl.when(tick == begin[k] + 1)
            def _():
                side.relay(0, k)

            on_head(tick, begin[k] + 1, lambda stream, c: stream.relay(c, k))

        @pl.when(tick == 0)
        def _():
            prepare()
            ask_all()

        @pl.when(tick == 1)
        def _():
            @pl.loop(0, res_rows)
            def _(row):
                resident(row)

        @pl.when((tick >= 2) & (tick < 2 + devices // batch))
        def _():
            @pl.loop(0, batch)
            def _(i):
                serve((tick - 2) * batch + i)

        @pl.when(tick == ready)
        def _():
            side.arrive(0)
            convolve()

            @pl.loop(0, res_rows)
            def _(row):
                update_resident(row)

        if GROUPS > 1:

            @pl.when(tick == landed_at)
            def _():
                @pl.loop(0, per_group)
                def _(c):
                    main[0].arrive(c)

            @pl.when(tick >= landed_at)
            def _():
                @pl.loop(0, share)
                def _(i):
                    child = (tick - landed_at) * share + i

                    @pl.when(child < child_dev)
                    def _():
                        update_child(child, 0)

    @pl.loop(1, devices)
    def _(step):
        d = (me + step) % devices
        replied(d).wait_recv()

    @pl.loop(0, child_dev)
    def _(child):
        value = o_in[plan[src_at + child]].astype(jnp.float32)
        put_attended(res_rows + child, jnp.where(plan[which_at + child] == 1, value[20:40], value[0:20]))

    @pl.loop(0, per_group)
    def _(c):
        main[-1].arrive(c)

    @pl.loop(0, child_dev)
    def _(child):
        update_child(child, GROUPS - 1)

    gated = []
    gates = g_v[...].astype(jnp.float32)
    lane = lax.broadcasted_iota(jnp.int32, (rows, 128), 1)
    total = jnp.zeros((rows, 128), jnp.float32)
    for t in range(STEPS):
        value = (carried[t] * read[t] + rest[t]) * silu(gates[:, t, :])
        gated.append(value)
        total = jnp.where(lane == t, jnp.sum(value * value, 1, keepdims=True), total)
    sums[...] = total

    def share_sums(d, slot):
        return pltpu.make_async_remote_copy(
            src_ref=sums, dst_ref=landed.at[slot], send_sem=psend.at[d], recv_sem=precv.at[slot],
            device_id=(me, d), device_id_type=MESH,
        )

    if peers > 1:

        @pl.loop(1, peers)
        def _(step):
            share_sums((tensor + step) % peers, tensor).start()

    for stream, count in [(side, 1)] + [(m, per_group) for m in main]:

        @pl.loop(0, count)
        def _(c):
            stream.finish(c)

    @pl.loop(1, devices)
    def _(step):
        d = (me + step) % devices
        ask(d).wait_send()
        reply(d).wait_send()

    if peers > 1:

        @pl.loop(1, peers)
        def _(step):
            d = (tensor + step) % peers
            share_sums(d, d).wait_recv()

        landed[tensor] = sums[...]
        total = landed[0]
        for d in range(1, peers):
            total = total + landed[d]
    scale = lax.rsqrt(total / INNER + EPSILON)
    row_of = lax.broadcasted_iota(jnp.int32, (rows, 128), 0)
    living = jnp.zeros((rows, 128), jnp.int32)
    for row in range(rows):
        living = jnp.where(row_of == row, alive[row], living)
    for t in range(STEPS):
        result = gated[t] * scale[:, t : t + 1] * gain_v[...]
        ssm_out[t] = jnp.where(living[:, 0:1] > 0, result, 0.0).astype(jnp.bfloat16)

    @pl.loop(0, rows)
    def _(row):
        for i in range(GROUPS):
            new_copy(row, i).wait()

    if peers > 1:

        @pl.loop(1, peers)
        def _(step):
            share_sums((tensor + step) % peers, tensor).wait_send()


def run_round(plan, scalars, arrays, ring, peers):
    slots = Slots(ring)
    half = ring // 2
    devices = COLUMNS * ring
    ssm, res, queries, gate = arrays[0], arrays[1], arrays[4], arrays[7]
    heads = ssm.shape[1]
    rows, res_rows = queries.shape[0], res.shape[0]
    child_dev = rows - res_rows
    features = heads * SSM_HEAD
    per_group = heads // GROUPS
    bf16, f32 = jnp.bfloat16, jnp.float32
    dma = pltpu.SemaphoreType.DMA

    def stream(count, height):
        return [
            pltpu.VMEM((count, ring - 1, NODE_DEV, height, STATE), bf16),
            pltpu.VMEM((count, slots.sent, height, STATE), bf16),
            pltpu.VMEM((count, slots.sent, height, STATE), bf16),
            pltpu.VMEM((count, slots.total, height, STATE), bf16),
            dma((count, 2, half)), dma((count, 2, half)),
            dma((count, 2, half + 1)), dma((count, 2, half + 1)),
            dma((count, 2, half)), dma((count, 2, half)),
        ]

    scratch = [pltpu.VMEM(a.shape, a.dtype) for a in arrays] + [dma((len(arrays),))]
    scratch += [
        pltpu.VMEM((rows, BLOCK, HEAD), bf16),
        pltpu.VMEM((NODE_DEV, 1, 16, STATE), bf16),
        pltpu.VMEM((rows, heads, SSM_HEAD, STATE), bf16),
        pltpu.VMEM((PAIR, PAIR), bf16),
        pltpu.VMEM((PAIR, PAIR), bf16),
        pltpu.VMEM((PAIR, PAIR), f32),
    ]
    taps = KERNEL - 1 + STEPS
    scratch += [
        pltpu.VMEM((taps, rows, features), f32),
        pltpu.VMEM((taps, rows, 2 * STATE), f32),
        pltpu.VMEM((16, rows, STATE), f32),
        pltpu.VMEM((16, rows, STATE), f32),
        pltpu.VMEM((16, rows, features), f32),
        pltpu.VMEM((STEPS, rows, features), f32),
        pltpu.VMEM((STEPS, rows, features), f32),
        pltpu.VMEM((STEPS, rows, features), f32),
    ]
    scratch += [
        pltpu.VMEM((devices, PAIR, HEAD), bf16),
        pltpu.VMEM((devices, PAIR, HEAD), bf16),
        pltpu.VMEM((devices, BACK, HEAD), bf16),
        pltpu.VMEM((devices, BACK, HEAD), bf16),
    ] + [dma((devices,))] * 4
    scratch += [
        pltpu.VMEM((rows, 128), f32),
        pltpu.VMEM((peers, rows, 128), f32),
        dma((peers,)),
        dma((peers,)),
        dma((rows, GROUPS)),
    ]
    for _ in range(GROUPS):
        scratch += stream(per_group, SSM_HEAD)
    scratch += stream(1, 16)
    smem = pl.BlockSpec(memory_space=pltpu.SMEM)
    vmem = pl.BlockSpec(memory_space=pltpu.VMEM)
    anywhere = pl.BlockSpec(memory_space=pl.ANY)
    return pl.pallas_call(
        functools.partial(round_kernel, slots, heads, res_rows, child_dev, peers),
        out_shape=[
            jax.ShapeDtypeStruct(queries.shape, bf16),
            jax.ShapeDtypeStruct((STEPS, rows, features), bf16),
            jax.ShapeDtypeStruct((rows,) + ssm.shape[1:], bf16),
        ],
        in_specs=[smem] * (1 + len(scalars)) + [anywhere] * len(arrays),
        out_specs=[vmem, vmem, anywhere],
        scratch_shapes=scratch,
        compiler_params=pltpu.CompilerParams(
            collective_id=0, has_side_effects=True, vmem_limit_bytes=60 * 1024 * 1024
        ),
        name="round",
    )(plan, *scalars, *arrays)


def per_device(
    ssm_resident, ssm_nodes, conv_resident, conv_nodes, convbc_resident, convbc_nodes,
    kv_resident, kv_nodes, len_resident, len_nodes, parents, alive_flags, queries, new_kv,
    x_in, gate_in, bc_in, dt_in, conv_x_weight, conv_bc_weight, a_log, dt_bias, skip_gain, norm_gain,
):
    devices = lax.axis_size("dp")
    me = lax.axis_index("dp")
    ring = devices // COLUMNS
    child_dev = parents.shape[0] // devices

    grouped = parents.reshape(devices, child_dev)
    match = (grouped // NODE_DEV)[:, None, :] == jnp.arange(devices)[None, :, None]
    tab = jnp.max(jnp.where(match, (grouped % NODE_DEV)[:, None, :], 0), axis=2).reshape(-1)
    own = lax.dynamic_slice_in_dim(parents, me * child_dev, child_dev)
    child_src = own // NODE_DEV
    mine = child_src[None, :] == jnp.arange(devices)[:, None]
    number = jnp.arange(child_dev)[None, :]
    first = jnp.min(jnp.where(mine, number, child_dev - 1), axis=1)
    second = jnp.max(jnp.where(mine, number, 0), axis=1)
    child_which = jnp.sum(jnp.where(mine & (number > first[:, None]), 1, 0), axis=0)
    relative = (
        (child_src // ring - me // ring) % COLUMNS * ring + (child_src % ring - me % ring) % ring
    )
    spot = jnp.arange(devices)[None, :] == relative[:, None]
    place = jnp.sum(jnp.where(spot, jnp.asarray(Slots(ring).table())[None, :], 0), axis=1)
    plan = jnp.concatenate([tab, first, second, child_src, child_which, place]).astype(jnp.int32)
    turned = [jnp.transpose(a, (1, 0, 2)) for a in (conv_resident, convbc_resident, conv_nodes, convbc_nodes)]
    arrays = [
        ssm_nodes, ssm_resident, kv_nodes, kv_resident, queries, new_kv, x_in, gate_in, bc_in,
        jnp.transpose(dt_in, (1, 2, 0)), *turned, conv_x_weight, conv_bc_weight, norm_gain[None, :],
    ]
    scalars = [len_nodes, len_resident, alive_flags, a_log, dt_bias, skip_gain]
    attn, ssm_out, new_ssm = run_round(plan, scalars, arrays, ring, lax.axis_size("tensor"))
    return attn, jnp.transpose(ssm_out, (1, 0, 2)), new_ssm


def solution(mesh):
    return jax.shard_map(
        per_device,
        mesh=mesh,
        in_specs=(
            P("dp", "tensor", None, None),
            P("dp", "tensor", None, None),
            P("dp", None, "tensor"),
            P("dp", None, "tensor"),
            P("dp", None, None),
            P("dp", None, None),
            P("dp", None, None, "tensor"),
            P("dp", None, None, "tensor"),
            P("dp"),
            P(),
            P(),
            P("dp"),
            P("dp", None, "tensor"),
            P("dp", None, None, "tensor"),
            P("dp", None, "tensor"),
            P("dp", None, "tensor"),
            P("dp", None, None),
            P("dp", None, "tensor"),
            P(None, "tensor"),
            P(),
            P("tensor"),
            P("tensor"),
            P("tensor"),
            P("tensor"),
        ),
        out_specs=(P("dp", None, "tensor"), P("dp", None, "tensor"), P("dp", "tensor", None, None)),
        check_vma=False,
    )
```

```python
import functools

import jax
import jax.numpy as jnp
import numpy as np
from jax import lax
from jax.experimental import pallas as pl
from jax.experimental.pallas import tpu as pltpu
from jax.sharding import PartitionSpec as P

HEAD = 128
SSM_HEAD = 64
STATE = 256
KERNEL = 4
STEPS = 4
INNER = 4096
EPSILON = 1e-05
NODE_DEV = 4
GROUP = 5
COLUMNS = 4
MESH = pl.DeviceIdType.MESH


class Slots:
    def __init__(self, ring):
        half = ring // 2
        self.ring, self.half = ring, half
        self.plus_direct, self.plus_transit = {0: 0}, {0: 1}
        self.minus_direct, self.minus_transit = {0: 0}, {}
        self.plus_group, self.minus_group = [(0, 2)], [(0, 1)]
        for k in range(1, half):
            start = 2 + 3 * (k - 1)
            self.plus_direct[k], self.plus_direct[ring - k], self.plus_transit[k] = start, start + 1, start + 2
            self.plus_group.append((start, 3))
            start = 1 + 3 * (k - 1)
            self.minus_direct[k], self.minus_direct[ring - k], self.minus_transit[ring - k] = start, start + 1, start + 2
            self.minus_group.append((start, 3))
        start = 2 + 3 * (half - 1)
        self.plus_direct[half] = start
        self.plus_group.append((start, 1))
        start = 1 + 3 * (half - 1)
        self.minus_direct[half], self.minus_transit[half] = start, start + 1
        self.minus_group.append((start, 2))
        self.sent = 3 * half
        self.plus = ring
        self.minus = ring + self.sent + half
        self.total = ring + 2 * (self.sent + half)

    def table(self):
        place = np.zeros((COLUMNS, self.ring), np.int32)
        for dz in range(self.ring):
            place[0, dz] = dz
            place[3, dz] = self.plus + self.plus_direct[dz]
            place[1, dz] = self.minus + self.minus_direct[dz]
            if dz < self.half:
                place[2, dz] = self.plus + self.sent + dz
            else:
                place[2, dz] = self.minus + self.sent + (self.ring - dz) - 1
        return place.reshape(-1)


PAIR = 64
BACK = 48
BLOCK = 32
RING_GROUPS = 2
ROUTE_HEADS = (2, 2, 2, 2)

SLOTS, X_SLOTS, X_START, LAG = 12, 11, 7, 3
REPLY = 0
STRIDE = 12
PLACE_ROW = 2 * (SLOTS + X_SLOTS)


def dot(a, b, dims):
    return lax.dot_general(a, b, (dims, ((), ())), preferred_element_type=jnp.float32)


def silu(value):
    return value / (1.0 + jnp.exp(-value))


def softplus(value):
    return jnp.maximum(value, 0.0) + jnp.log1p(jnp.exp(-jnp.abs(value)))


def split(value, parts):
    pieces = []
    for _ in range(parts):
        piece = value.astype(jnp.bfloat16).astype(jnp.float32)
        pieces.append(piece)
        value = value - piece
    return pieces


def round_kernel(
    slots, heads, res_rows, child_dev, peers, routed,
    plan, routes, len_nodes, len_res, alive, a_log, dt_bias, skip_gain,
    ssm_h, res_h, kvn_h, kvr_h, q_h, nkv_h, x_h, g_h, bc_h, dt_h, cr_h, cbr_h, cn_h, cbn_h, wx_h, wbc_h, gain_h,
    att, ssm_out, new_out,
    *scratch,
):
    scratch = list(scratch)

    def take(count):
        taken, scratch[:count] = scratch[:count], []
        return taken

    loaded = take(17)
    (ssm, res, kv_nodes, kv_res, q_v, nkv_v, x_v, g_v, bc_v, dt_v, cr_v, cbr_v, cn_v, cbn_v, wx_v, wbc_v, gain_v) = loaded
    (load_sem,) = take(1)
    comb, convp, new_v, gather, shift, bias = take(6)
    ux, ub, c_parts, b_parts, w_parts, carried, rest, read = take(8)
    q_out, q_in, o_out, o_in = take(4)
    qsend, qrecv, rsend, rrecv = take(4)
    sums, landed, psend, precv = take(4)
    (new_sem,) = take(1)

    ring, half = slots.ring, slots.half
    groups = len(ROUTE_HEADS) if routed else RING_GROUPS
    devices = COLUMNS * ring
    rows = res_rows + child_dev
    features = heads * SSM_HEAD
    me = lax.axis_index("dp")
    tensor = lax.axis_index("tensor")
    x, z = me // ring, me % ring
    first_at = devices * devices
    second_at = first_at + devices
    src_at = second_at + devices
    which_at = src_at + child_dev
    place_at = which_at + child_dev

    sources = (ssm_h, res_h, kvn_h, kvr_h, q_h, nkv_h, x_h, g_h, bc_h, dt_h, cr_h, cbr_h, cn_h, cbn_h, wx_h, wbc_h, gain_h)
    loads = [pltpu.make_async_copy(a, b, load_sem.at[i]) for i, (a, b) in enumerate(zip(sources, loaded))]
    for load in loads:
        load.start()

    barrier = pltpu.get_barrier_semaphore()

    @pl.loop(1, devices)
    def _(step):
        pl.semaphore_signal(
            barrier, inc=1, device_id=((me + step) % devices, tensor), device_id_type=MESH
        )

    if peers > 1:

        @pl.loop(1, peers)
        def _(step):
            pl.semaphore_signal(
                barrier, inc=1, device_id=(me, (tensor + step) % peers), device_id_type=MESH
            )

    for load in loads:
        load.wait()

    def at(column, row):
        return ((column + COLUMNS) % COLUMNS) * ring + (row + ring) % ring

    above, below = at(x, z + 1), at(x, z - 1)
    right, left = at(x + 1, z), at(x - 1, z)
    across = at(x + 2, z)

    for node in range(NODE_DEV):
        lines = []
        for value in (cn_v, cbn_v):
            for j in range(KERNEL - 1):
                for begin in range(0, value.shape[2], STATE):
                    lines.append(value[j].astype(jnp.float32)[node : node + 1, begin : begin + STATE])
        used = len(lines)
        lines.append(jnp.zeros((16 - used, STATE), jnp.float32))
        convp[node, 0] = jnp.concatenate(lines, 0).astype(jnp.bfloat16)
    x_lines = (KERNEL - 1) * features // STATE

    pl.semaphore_wait(barrier, devices - 1 + peers - 1)

    def send(source, target, send_sem, recv_sem, device):
        return pltpu.make_async_remote_copy(
            src_ref=source,
            dst_ref=target,
            send_sem=send_sem,
            recv_sem=recv_sem,
            device_id=(device, tensor),
            device_id_type=MESH,
        )

    class Stream:
        def __init__(self, own, base, refs):
            self.own, self.base, self.count = own, base, refs[0].shape[0]
            (self.gz, self.sp, self.sm, self.arr,
             self.zsend, self.zrecv, self.xsend, self.xrecv, self.fsend, self.frecv) = refs

        def hop(self, c, k, up):
            if k == 1:
                source = self.own.at[:, self.base + c]
            else:
                source = self.gz.at[c, (ring - k + 1 if up else k - 1) - 1]
            target = self.gz.at[c, (ring - k if up else k) - 1]
            if k == half:
                nodes = pl.ds(0 if up else NODE_DEV // 2, NODE_DEV // 2)
                source, target = source.at[nodes], target.at[nodes]
            way = 0 if up else 1
            return send(
                source, target, self.zsend.at[c, way, k - 1], self.zrecv.at[c, way, k - 1],
                above if up else below,
            )

        def across_x(self, c, k, plus):
            start, size = (slots.plus_group if plus else slots.minus_group)[k]
            base = slots.plus if plus else slots.minus
            way = 0 if plus else 1
            return send(
                (self.sp if plus else self.sm).at[c, pl.ds(start, size)],
                self.arr.at[c, pl.ds(base + start, size)],
                self.xsend.at[c, way, k], self.xrecv.at[c, way, k],
                right if plus else left,
            )

        def forward(self, c, k, plus):
            if plus:
                source = slots.plus + slots.plus_transit[k]
                target = slots.plus + slots.sent + k
                index = k
            else:
                source = slots.minus + slots.minus_transit[half if k == half else ring - k]
                target = slots.minus + slots.sent + k - 1
                index = k - 1
            way = 0 if plus else 1
            return send(
                self.arr.at[c, source], self.arr.at[c, target],
                self.fsend.at[c, way, index], self.frecv.at[c, way, index],
                right if plus else left,
            )

        def pick(self, c, dz, target):
            node = plan[target * devices + at(x, z + dz)]
            if dz == 0:
                return self.own[node, self.base + c]
            picked = self.gz[c, dz - 1, 0]
            for other in range(1, NODE_DEV):
                picked = jnp.where(node == other, self.gz[c, dz - 1, other], picked)
            return picked

        def group(self, c, k):
            dzs = [0] if k == 0 else [half] if k == half else [k, ring - k]
            for dz in dzs:
                self.sp[c, slots.plus_direct[dz]] = self.pick(c, dz, right)
                self.sm[c, slots.minus_direct[dz]] = self.pick(c, dz, left)
                if dz in slots.plus_transit:
                    self.sp[c, slots.plus_transit[dz]] = self.pick(c, dz, across)
                else:
                    self.sm[c, slots.minus_transit[dz]] = self.pick(c, dz, across)
            self.across_x(c, k, True).start()
            self.across_x(c, k, False).start()
            for dz in dzs:
                self.arr[c, dz] = self.pick(c, dz, me)

        def stage(self, c, k):
            for up in (True, False):
                if k >= 1:
                    self.hop(c, k, up).wait_recv()
                if k < half:
                    self.hop(c, k + 1, up).start()
            self.group(c, k)

        def relay(self, c, k):
            for plus in (True, False):
                self.across_x(c, k, plus).wait_recv()
                if k in (range(half) if plus else range(1, half + 1)):
                    self.forward(c, k, plus).start()

        def arrive(self, c):
            for k in range(half + 1):
                for plus in (True, False):
                    if k in (range(half) if plus else range(1, half + 1)):
                        self.forward(c, k, plus).wait_recv()

        def finish(self, c):
            for k in range(1, half + 1):
                for up in (True, False):
                    self.hop(c, k, up).wait_send()
            for k in range(half + 1):
                for plus in (True, False):
                    self.across_x(c, k, plus).wait_send()
                    if k in (range(half) if plus else range(1, half + 1)):
                        self.forward(c, k, plus).wait_send()

    class Route:
        def __init__(self, own, base, count, refs):
            self.own, self.base, self.count = own, base, count
            self.inn, self.out, self.zsend, self.zrecv, self.xsend, self.xrecv = refs

        def copy(self, way, slot):
            start = (0, SLOTS, 2 * SLOTS, 2 * SLOTS + X_SLOTS)[way]
            if way < 2:
                sems = self.zsend.at[way, slot], self.zrecv.at[way, slot]
            else:
                sems = self.xsend.at[way - 2, slot], self.xrecv.at[way - 2, slot]
            return send(
                self.out.at[start + slot], self.inn.at[start + slot], *sems,
                (above, below, right, left)[way],
            )

        def first(self, code):
            node = jnp.minimum(code, NODE_DEV - 1)
            return tuple(self.own[node, self.base + h] for h in range(self.count))

        def choose(self, code, slot, held):
            return tuple(
                jnp.where(code == NODE_DEV + slot, self.inn[slot, h], held[h]) for h in range(self.count)
            )

        def put(self, way, slot, value):
            start = (0, SLOTS, 2 * SLOTS, 2 * SLOTS + X_SLOTS)[way]
            for h in range(self.count):
                self.out[start + slot, h] = value[h]
            self.copy(way, slot).start()

        def z_step(self, step):
            landed = step - LAG

            @pl.when((landed >= 0) & (landed < SLOTS))
            def _():
                for way in (0, 1):
                    self.copy(way, landed).wait_recv()

            @pl.when((step >= 0) & (step < SLOTS))
            def _():
                for way in (0, 1):
                    code = routes[way * SLOTS + step, me]
                    value = lax.fori_loop(
                        0, jnp.maximum(step - LAG + 1, 0),
                        lambda r, held: self.choose(code, way * SLOTS + r, held), self.first(code),
                    )
                    self.put(way, step, value)

        def x_step(self, step):
            slot = step - X_START
            landed = slot - LAG

            @pl.when((landed >= 0) & (landed < X_SLOTS))
            def _():
                for way in (2, 3):
                    self.copy(way, landed).wait_recv()

            @pl.when((slot >= 0) & (slot < X_SLOTS))
            def _():
                codes = [routes[2 * SLOTS + i * X_SLOTS + slot, me] for i in range(2)]

                def from_z(r, held):
                    result = []
                    for code, value in zip(codes, held):
                        for start in (0, SLOTS):
                            value = self.choose(code, start + r, value)
                        result.append(value)
                    return tuple(result)

                def from_x(r, held):
                    return tuple(
                        self.choose(codes[i], 2 * SLOTS + i * X_SLOTS + r, held[i]) for i in range(2)
                    )

                held = tuple(self.first(code) for code in codes)
                held = lax.fori_loop(0, jnp.minimum(step - LAG + 1, SLOTS), from_z, held)
                held = lax.fori_loop(0, jnp.maximum(landed + 1, 0), from_x, held)
                for i in range(2):
                    self.put(2 + i, slot, held[i])

        def arrived(self, child):
            code = routes[PLACE_ROW + child, me]
            slot = jnp.maximum(code - NODE_DEV, 0)
            held = self.first(code)
            return [jnp.where(code < NODE_DEV, held[h], self.inn[slot, h]) for h in range(self.count)]

        def finish(self, _):
            @pl.loop(0, SLOTS)
            def _(slot):
                for way in (0, 1):
                    self.copy(way, slot).wait_send()

            @pl.loop(0, X_SLOTS)
            def _(slot):
                for way in (2, 3):
                    self.copy(way, slot).wait_send()

    per_group = heads // groups
    if routed:
        main = [Route(ssm, sum(ROUTE_HEADS[:i]), ROUTE_HEADS[i], take(6)) for i in range(groups)]
        side = Route(convp, 0, 1, take(6))
    else:
        main = [Stream(ssm, i * per_group, take(10)) for i in range(groups)]
        side = Stream(convp, 0, take(10))

    def on_head(tick, offset, act):
        c = tick - offset
        for i in range(groups):

            @pl.when((c >= i * per_group) & (c < (i + 1) * per_group))
            def _():
                act(main[i], c - i * per_group)

    def weigh(weights, values):
        high = weights.astype(jnp.bfloat16)
        low = (weights - high.astype(jnp.float32)).astype(jnp.bfloat16)
        return dot(high, values, ((1,), (0,))) + dot(low, values, ((1,), (0,)))

    def attend(message, keys, values, length):
        scale = HEAD**-0.5
        old = dot(message, keys, ((1,), (1,))) * scale
        spot = lax.broadcasted_iota(jnp.int32, old.shape, 1)
        old = jnp.where(spot < length, old, -jnp.inf)
        moved = dot(shift[...], message, ((1,), (0,))).astype(jnp.bfloat16)
        new = dot(message, moved, ((1,), (1,))) * scale + bias[...]
        top = jnp.maximum(jnp.max(old, 1, keepdims=True), jnp.max(new, 1, keepdims=True))
        old, new = jnp.exp(old - top), jnp.exp(new - top)
        total = jnp.sum(old, 1, keepdims=True) + jnp.sum(new, 1, keepdims=True)
        return (weigh(old, values) + weigh(new, message)) / total

    def pack(first, second):
        both = jnp.concatenate([comb[first], comb[second]], 0)
        return dot(gather[...], both, ((1,), (0,))).astype(jnp.bfloat16)

    def asking(d):
        return send(q_out.at[d], q_in.at[me], qsend.at[d], qrecv.at[me], d)

    def asked(d):
        return send(q_out.at[d], q_in.at[d], qsend.at[d], qrecv.at[d], d)

    def reply(d):
        return send(o_out.at[d], o_in.at[me], rsend.at[d], rrecv.at[me], d)

    def replied(d):
        return send(o_out.at[d], o_in.at[d], rsend.at[d], rrecv.at[d], d)

    def prepare():
        r = lax.broadcasted_iota(jnp.int32, (PAIR, PAIR), 0)
        c = lax.broadcasted_iota(jnp.int32, (PAIR, PAIR), 1)
        query = r + jnp.where(r >= 20, 12, 0)
        key = r - 20 + jnp.where(r >= 44, 28, 0)
        value = r - 24 + jnp.where(r >= 52, 28, 0)
        column = jnp.where(r < 40, query, jnp.where(r < 48, key, jnp.where(r < 56, value, -1)))
        gather[...] = jnp.where(column == c, 1.0, 0.0).astype(jnp.bfloat16)
        shift[...] = jnp.where((r >= 48) & (r < 56) & (c == r - 8), 1.0, 0.0).astype(jnp.bfloat16)
        same = jnp.where(c >= 52, 1, 0) == jnp.where(r >= 20, 1, 0)
        seen = (r < 40) & (c >= 48) & (c < 56) & same & ((c & 3) <= (r & 3))
        bias[...] = jnp.where(seen, 0.0, -jnp.inf)

        @pl.loop(0, rows)
        def _(row):
            query = q_v[row].astype(jnp.float32)
            lines = [query[:, g * HEAD : (g + 1) * HEAD] for g in range(GROUP)]
            fresh = nkv_v[row].astype(jnp.float32)
            lines += [fresh[0], fresh[1], jnp.zeros((4, HEAD), jnp.float32)]
            comb[row] = jnp.concatenate(lines, 0).astype(jnp.bfloat16)

    def ask(steps):
        messages = []
        for step in steps:
            d = (me + step) % devices
            messages.append(pack(res_rows + plan[first_at + d], res_rows + plan[second_at + d]))
        for step, message in zip(steps, messages):
            d = (me + step) % devices

            @pl.when(step == 0)
            def _():
                q_in[me] = message

            @pl.when(step != 0)
            def _():
                q_out[d] = message
                asking(d).start()

    def serve(steps):
        served = [(me + devices - step) % devices for step in steps]
        for step, d in zip(steps, served):

            @pl.when(step != 0)
            def _():
                asked(d).wait_recv()

        results = []
        for d in served:
            node = plan[d * devices + me]
            length = len_nodes[me * NODE_DEV + node]
            result = attend(q_in[d], kv_nodes[node, 0], kv_nodes[node, 1], length)
            results.append(result[:BACK].astype(jnp.bfloat16))
        for step, d, result in zip(steps, served, results):

            @pl.when(step == 0)
            def _():
                o_in[me] = result

            @pl.when(step != 0)
            def _():
                o_out[d] = result
                if not routed:
                    reply(d).start()

    def put_attended(row, value):
        value = jnp.where(alive[row] > 0, value, 0.0).astype(jnp.bfloat16)
        for g in range(GROUP):
            att[row, :, g * HEAD : (g + 1) * HEAD] = value[4 * g : 4 * g + 4]

    def resident(lines):
        messages = [pack(row, row) for row in lines]
        results = [
            attend(message, kv_res[row, 0], kv_res[row, 1], len_res[row])[:20]
            for row, message in zip(lines, messages)
        ]
        for row, result in zip(lines, results):
            put_attended(row, result)

    def convolve():
        for j in range(KERNEL - 1):
            ux[j, 0:res_rows] = cr_v[j].astype(jnp.float32)
            ub[j, 0:res_rows] = cbr_v[j].astype(jnp.float32)
        for child in range(child_dev):
            if routed:
                lines = side.arrived(child)[0].astype(jnp.float32)
            else:
                lines = side.arr[0, plan[place_at + child]].astype(jnp.float32)
            at_row = slice(res_rows + child, res_rows + child + 1)
            line = 0
            for target in (ux, ub):
                for j in range(KERNEL - 1):
                    for begin in range(0, target.shape[2], STATE):
                        target[j, at_row, begin : begin + STATE] = lines[line : line + 1]
                        line += 1
        fresh_x = x_v[...].astype(jnp.float32)
        fresh_b = bc_v[...].astype(jnp.float32)
        for t in range(STEPS):
            ux[KERNEL - 1 + t] = fresh_x[:, t, :]
            ub[KERNEL - 1 + t] = fresh_b[:, t, :]
        weights_x = wx_v[...].astype(jnp.float32)
        weights_b = wbc_v[...].astype(jnp.float32)

        def mix(source, weights, t):
            total = weights[0:1] * source[t]
            for tap in range(1, KERNEL):
                total = total + weights[tap : tap + 1] * source[t + tap]
            return silu(total)

        lane = lax.broadcasted_iota(jnp.int32, (1, features), 1)

        def spread(table):
            value = jnp.zeros((1, features), jnp.float32)
            for h in range(heads):
                inside = (lane >= h * SSM_HEAD) & (lane < (h + 1) * SSM_HEAD)
                value = jnp.where(inside, table[h], value)
            return value

        rate, offset, skip = -jnp.exp(spread(a_log)), spread(dt_bias), spread(skip_gain)
        head = lax.broadcasted_iota(jnp.int32, (heads, features), 0) * SSM_HEAD
        lanes = lax.broadcasted_iota(jnp.int32, (heads, features), 1)
        one_hot = jnp.where((lanes >= head) & (lanes < head + SSM_HEAD), 1.0, 0.0).astype(jnp.bfloat16)
        b_list = []
        c_parts[...] = jnp.zeros(c_parts.shape, jnp.float32)
        b_parts[...] = jnp.zeros(b_parts.shape, jnp.float32)
        w_parts[...] = jnp.zeros(w_parts.shape, jnp.float32)
        since = []
        for t in range(STEPS):
            both = mix(ub, weights_b, t)
            b, c = both[:, :STATE], both[:, STATE:]
            b_list.append(b)
            for part, piece in enumerate(split(c, 3)):
                c_parts[part * 4 + t] = piece
            high, low = split(b, 2)
            b_parts[t], b_parts[4 + t], b_parts[8 + t] = high, low, high
            dt = softplus(dot(dt_v[t], one_hot, ((0,), (0,))) + offset)
            decay = jnp.exp(rate * dt)
            mixed = mix(ux, weights_x, t)
            carried[t] = decay if t == 0 else carried[t - 1] * decay
            since = [value * decay for value in since] + [dt * mixed]
            total = skip * mixed
            for s in range(t + 1):
                total = total + since[s] * jnp.sum(c * b_list[s], 1, keepdims=True)
            rest[t] = total
        for s in range(STEPS):
            high, low = split(since[s], 2)
            w_parts[s], w_parts[4 + s], w_parts[8 + s] = high, high, low

    def new_copy(row, i):
        span = pl.ds(main[i].base, main[i].count)
        return pltpu.make_async_copy(new_v.at[row, span], new_out.at[row, span], new_sem.at[row, i])

    def update(row, i, state):
        base, count = main[i].base, main[i].count
        span = slice(base * SSM_HEAD, (base + count) * SSM_HEAD)
        width = count * SSM_HEAD
        here = pl.ds(row, 1)
        state = state.reshape(width, STATE)
        c_row = c_parts[:, here, :].reshape(16, STATE).astype(jnp.bfloat16)
        b_row = b_parts[:, here, :].reshape(16, STATE).astype(jnp.bfloat16)
        window = span.start // STATE * STATE
        w_row = w_parts[:, here, window : max(window + STATE, span.stop)]
        w_row = w_row[:, :, span.start - window : span.stop - window].reshape(16, width).astype(jnp.bfloat16)
        got = dot(c_row, state, ((1,), (1,)))
        got = got[0:4] + got[4:8] + got[8:12]
        read[row, 0:STEPS, span] = got
        added = dot(w_row, b_row, ((0,), (0,)))
        last = carried[STEPS - 1 : STEPS, here, window : max(window + STATE, span.stop)]
        last = last.reshape(1, last.shape[2])[:, span.start - window : span.stop - window]
        for h in range(count):
            part = slice(h * SSM_HEAD, (h + 1) * SSM_HEAD)
            factor = last[:, h * SSM_HEAD : h * SSM_HEAD + 1]
            new = factor * state[part].astype(jnp.float32) + added[part]
            new_v[row, base + h] = new.astype(jnp.bfloat16)
    def update_resident(lines):
        for row in lines:
            for i in range(groups):
                update(row, i, res[row, main[i].base : main[i].base + main[i].count])
        for row in lines:
            for i in range(groups):
                new_copy(row, i).start()

    def update_child(children, i):
        for child in children:
            if routed:
                state = jnp.stack(main[i].arrived(child))
            else:
                state = main[i].arr[:, plan[place_at + child]]
            update(res_rows + child, i, state)
        for child in children:
            new_copy(res_rows + child, i).start()

    def spread_over(tick, start, per_tick, total, act):
        steps = -(-total // per_tick)

        @pl.when((tick >= start) & (tick < start + steps))
        def _():
            act([(tick - start) * per_tick + j for j in range(per_tick)])

    def reply_all():
        @pl.loop(1, devices)
        def _(step):
            reply((me + devices - step) % devices).start()

    def gather_replies():
        @pl.loop(1, devices)
        def _(step):
            replied((me + step) % devices).wait_recv()

        @pl.loop(0, child_dev)
        def _(child):
            value = o_in[plan[src_at + child]].astype(jnp.float32)
            put_attended(res_rows + child, jnp.where(plan[which_at + child] == 1, value[20:40], value[0:20]))

    def run_ring():
        batch = 4
        begin = [2 * k for k in range(half + 1)]
        ticks = heads + begin[half] + 1
        ready = begin[half] + 2
        landed_at = per_group + begin[half] + 1
        share = -(-child_dev // (ticks - landed_at))

        @pl.loop(0, ticks)
        def _(tick):
            for k in range(half, -1, -1):

                @pl.when(tick == begin[k])
                def _():
                    side.stage(0, k)

                on_head(tick, begin[k], lambda stream, c: stream.stage(c, k))
            for k in range(half, -1, -1):

                @pl.when(tick == begin[k] + 1)
                def _():
                    side.relay(0, k)

                on_head(tick, begin[k] + 1, lambda stream, c: stream.relay(c, k))

            @pl.when(tick == 0)
            def _():
                prepare()
                pl.loop(0, devices)(lambda step: ask([step]))

            @pl.when(tick == 1)
            def _():
                @pl.loop(0, res_rows)
                def _(row):
                    resident([row])

            @pl.when((tick >= 2) & (tick < 2 + devices // batch))
            def _():
                @pl.loop(0, batch)
                def _(i):
                    serve([(tick - 2) * batch + i])

            @pl.when(tick == ready)
            def _():
                side.arrive(0)
                convolve()

                @pl.loop(0, res_rows)
                def _(row):
                    update_resident([row])

            if groups > 1:

                @pl.when(tick == landed_at)
                def _():
                    @pl.loop(0, per_group)
                    def _(c):
                        main[0].arrive(c)

                @pl.when(tick >= landed_at)
                def _():
                    @pl.loop(0, share)
                    def _(i):
                        child = (tick - landed_at) * share + i

                        @pl.when(child < child_dev)
                        def _():
                            update_child([child], 0)

        @pl.loop(0, per_group)
        def _(c):
            main[-1].arrive(c)

    def run_routes():
        span = X_START + X_SLOTS + LAG
        children = span + 1 + -(-res_rows // 2)
        serve_from = 8
        wait = -(-child_dev // 4)
        ticks = (groups - 1) * STRIDE + span

        @pl.loop(0, ticks)
        def _(tick):
            for i in range(groups):
                main[i].z_step(tick - i * STRIDE)
            side.z_step(tick)
            for i in range(groups):
                main[i].x_step(tick - i * STRIDE)
            side.x_step(tick)
            pl.when(tick == 0)(prepare)
            spread_over(tick, 1, 1, devices, ask)
            spread_over(tick, 9, 4, res_rows, resident)
            spread_over(tick, serve_from, 1, devices, serve)
            pl.when(tick == span)(convolve)
            spread_over(tick, span + 1, 2, res_rows, update_resident)
            for i in range(groups - 1):
                start = max(children + i * wait, i * STRIDE + span)
                spread_over(tick, start, 4, child_dev, functools.partial(update_child, i=i))
            pl.when(tick == ticks - span + SLOTS + REPLY)(reply_all)

    if routed:
        run_routes()
    else:
        run_ring()

    @pl.loop(0, child_dev // 4)
    def _(part):
        update_child([4 * part + j for j in range(4)], groups - 1)

    gated = []
    gates = g_v[...].astype(jnp.float32)
    reads = read[...]
    lane = lax.broadcasted_iota(jnp.int32, (rows, 128), 1)
    total = jnp.zeros((rows, 128), jnp.float32)
    for t in range(STEPS):
        value = (carried[t] * reads[:, t, :] + rest[t]) * silu(gates[:, t, :])
        gated.append(value)
        total = jnp.where(lane == t, jnp.sum(value * value, 1, keepdims=True), total)
    sums[...] = total

    def share_sums(d, slot):
        return pltpu.make_async_remote_copy(
            src_ref=sums, dst_ref=landed.at[slot], send_sem=psend.at[d], recv_sem=precv.at[slot],
            device_id=(me, d), device_id_type=MESH,
        )

    if peers > 1:

        @pl.loop(1, peers)
        def _(step):
            share_sums((tensor + step) % peers, tensor).start()

    gather_replies()
    for stream, count in [(side, 1)] + [(m, 1 if routed else per_group) for m in main]:

        @pl.loop(0, count)
        def _(c):
            stream.finish(c)

    @pl.loop(1, devices)
    def _(step):
        d = (me + step) % devices
        asking(d).wait_send()
        reply(d).wait_send()

    if peers > 1:

        @pl.loop(1, peers)
        def _(step):
            d = (tensor + step) % peers
            share_sums(d, d).wait_recv()

        landed[tensor] = sums[...]
        total = landed[0]
        for d in range(1, peers):
            total = total + landed[d]
    scale = lax.rsqrt(total / INNER + EPSILON)
    row_of = lax.broadcasted_iota(jnp.int32, (rows, 128), 0)
    living = jnp.zeros((rows, 128), jnp.int32)
    for row in range(rows):
        living = jnp.where(row_of == row, alive[row], living)
    for t in range(STEPS):
        result = gated[t] * scale[:, t : t + 1] * gain_v[...]
        ssm_out[t] = jnp.where(living[:, 0:1] > 0, result, 0.0).astype(jnp.bfloat16)

    @pl.loop(0, rows)
    def _(row):
        for i in range(groups):
            new_copy(row, i).wait()

    if peers > 1:

        @pl.loop(1, peers)
        def _(step):
            share_sums((tensor + step) % peers, tensor).wait_send()


def run_round(plan, routes, scalars, arrays, ring, peers, routed):
    slots = Slots(ring)
    half = ring // 2
    devices = COLUMNS * ring
    ssm, res, queries, gate = arrays[0], arrays[1], arrays[4], arrays[7]
    heads = ssm.shape[1]
    rows, res_rows = queries.shape[0], res.shape[0]
    child_dev = rows - res_rows
    features = heads * SSM_HEAD
    groups = len(ROUTE_HEADS) if routed else RING_GROUPS
    per_group = heads // groups
    bf16, f32 = jnp.bfloat16, jnp.float32
    dma = pltpu.SemaphoreType.DMA

    def stream(count, height):
        return [
            pltpu.VMEM((count, ring - 1, NODE_DEV, height, STATE), bf16),
            pltpu.VMEM((count, slots.sent, height, STATE), bf16),
            pltpu.VMEM((count, slots.sent, height, STATE), bf16),
            pltpu.VMEM((count, slots.total, height, STATE), bf16),
            dma((count, 2, half)), dma((count, 2, half)),
            dma((count, 2, half + 1)), dma((count, 2, half + 1)),
            dma((count, 2, half)), dma((count, 2, half)),
        ]

    scratch = [pltpu.VMEM(a.shape, a.dtype) for a in arrays] + [dma((len(arrays),))]
    scratch += [
        pltpu.VMEM((rows, BLOCK, HEAD), bf16),
        pltpu.VMEM((NODE_DEV, 1, 16, STATE), bf16),
        pltpu.VMEM((rows, heads, SSM_HEAD, STATE), bf16),
        pltpu.VMEM((PAIR, PAIR), bf16),
        pltpu.VMEM((PAIR, PAIR), bf16),
        pltpu.VMEM((PAIR, PAIR), f32),
    ]
    taps = KERNEL - 1 + STEPS
    scratch += [
        pltpu.VMEM((taps, rows, features), f32),
        pltpu.VMEM((taps, rows, 2 * STATE), f32),
        pltpu.VMEM((16, rows, STATE), f32),
        pltpu.VMEM((16, rows, STATE), f32),
        pltpu.VMEM((16, rows, features), f32),
        pltpu.VMEM((STEPS, rows, features), f32),
        pltpu.VMEM((STEPS, rows, features), f32),
        pltpu.VMEM((rows, 8, features), f32),
    ]
    scratch += [
        pltpu.VMEM((devices, PAIR, HEAD), bf16),
        pltpu.VMEM((devices, PAIR, HEAD), bf16),
        pltpu.VMEM((devices, BACK, HEAD), bf16),
        pltpu.VMEM((devices, BACK, HEAD), bf16),
    ] + [dma((devices,))] * 4
    scratch += [
        pltpu.VMEM((rows, 128), f32),
        pltpu.VMEM((peers, rows, 128), f32),
        dma((peers,)),
        dma((peers,)),
        dma((rows, groups)),
    ]
    def route(count, height):
        packets = 2 * (SLOTS + X_SLOTS)
        return [
            pltpu.VMEM((packets, count, height, STATE), bf16),
            pltpu.VMEM((packets, count, height, STATE), bf16),
            dma((2, SLOTS)), dma((2, SLOTS)), dma((2, X_SLOTS)), dma((2, X_SLOTS)),
        ]

    for _ in range(groups):
        scratch += route(ROUTE_HEADS[_], SSM_HEAD) if routed else stream(per_group, SSM_HEAD)
    scratch += (route if routed else stream)(1, 16)
    smem = pl.BlockSpec(memory_space=pltpu.SMEM)
    vmem = pl.BlockSpec(memory_space=pltpu.VMEM)
    anywhere = pl.BlockSpec(memory_space=pl.ANY)
    return pl.pallas_call(
        functools.partial(round_kernel, slots, heads, res_rows, child_dev, peers, routed),
        out_shape=[
            jax.ShapeDtypeStruct(queries.shape, bf16),
            jax.ShapeDtypeStruct((STEPS, rows, features), bf16),
            jax.ShapeDtypeStruct((rows,) + ssm.shape[1:], bf16),
        ],
        in_specs=[smem] * (2 + len(scalars)) + [anywhere] * len(arrays),
        out_specs=[vmem, vmem, anywhere],
        scratch_shapes=scratch,
        compiler_params=pltpu.CompilerParams(
            collective_id=1 if routed else 0, has_side_effects=True, vmem_limit_bytes=60 * 1024 * 1024
        ),
        name="routed_round" if routed else "ring_round",
    )(plan, routes, *scalars, *arrays)


def plan_routes(parents, ops, S, L, X0, NX):
    where, rollx, rollz, srl, orall, const, lanes = ops
    x, z = (lanes >> 3) & 3, lanes & 7
    kids = []
    zero = const(0)
    need = [zero, zero, zero, zero]
    for p in parents:
        src, n = p >> 2, p & 3
        dx, dz = ((src >> 3) - x) & 3, ((src & 7) - z) & 7
        bit = const(1) << (n * 8 + dz)
        kids.append((dx, dz, n, bit))
        for k in range(4):
            need[k] = need[k] | where(dx == k, bit, zero)
    need = [orall(v) for v in need]
    me_, across, right, left = need[0], rollx(need[2], 2), rollx(need[3], -1), rollx(need[1], 1)
    row = me_ | across | right | left
    D4, D5, D3 = 0x10101010, 0x20202020, 0x08080808
    UPB, DNB = 0xE0E0E0E0 - (1 << 32), 0x0E0E0E0E
    D0 = 0x01010101
    ev = 0x00100010
    opp = row & D4
    up_near, dn_near = zero, zero
    go_up, go_dn = zero, zero
    from_below, from_above = row, row
    for k in (1, 2, 3):
        from_below, from_above = rollz(from_below, 1), rollz(from_above, -1)
        up_near = up_near | (srl(from_below, k) & opp)
        dn_near = dn_near | ((from_above << k) & opp)
        go_up = go_up | (up_near & ~dn_near)
        go_dn = go_dn | (dn_near & ~up_near)
    go_up = go_up | (opp & ~go_dn & ev)
    need_up = (row & UPB) | go_up
    need_dn = (row & DNB) | (opp & ~go_up)

    def sender_up(m):
        return srl(m & (0x80808080 - (1 << 32)), 7) & D0 | ((m & 0x70707070) << 1)

    def receiver_up(m):
        return ((m & D0) << 7) | srl(m & UPB, 1)

    def sender_dn(m):
        return srl(m & (DNB | D4), 1)

    def receiver_dn(m):
        return m << 1

    todo_all = zero
    C, U = {}, {}
    for name, wanted, step, send, recv, keep in (
        ("up", need_up, 1, sender_up, receiver_up, UPB),
        ("dn", need_dn, -1, sender_dn, receiver_dn, DNB),
    ):
        A = [send(rollz(wanted, -step))]
        for _ in range(3):
            A.append(send(rollz(A[-1] & keep, -step)))
        act = A[0] | A[1] | A[2] | A[3]
        ready = act & D0
        todo = act
        come = {}
        C[name], U[name] = [], []
        for s in range(S):
            if s in come:
                ready = ready | (come[s] & act)
            best = ready & A[3]
            for k in (2, 1, 0):
                best = where(best != 0, best, ready & A[k])
            pick = best & -best
            ready = ready & ~pick
            todo = todo & ~pick
            got = rollz(recv(pick), step)
            C[name].append(pick)
            U[name].append(got)
            come[s + L] = got
        todo_all = todo_all | todo
    EVEN = 0x55555555
    first_p = (across & right) | (across & ~left & EVEN)
    first_m = across & ~first_p
    direct_p, direct_m = right & ~first_p, left & ~first_m
    X = {}
    for name, step, direct, first in (("p", 1, direct_p, first_p), ("m", -1, direct_m, first_m)):
        arrived = {}
        second = rollx(first, step)
        todo1, todo2, todod = first, second, direct
        have = D0 | zero
        got2 = zero
        come = {}
        X[name] = []
        for t in range(X0 + NX):
            s = t - L
            if 0 <= s < S:
                have = have | U["up"][s] | U["dn"][s]
            if t in come:
                got2 = got2 | come[t]
            if t < X0:
                continue
            r1, r2, rd = todo1 & have, todo2 & got2, todod & have
            p1 = r1 & -r1
            none = r1 == 0
            p2 = where(none, r2 & -r2, zero)
            none = none & (r2 == 0)
            pd = where(none, rd & -rd, zero)
            todo1, todo2, todod = todo1 & ~p1, todo2 & ~p2, todod & ~pd
            come[t + L] = rollx(p1, step)
            X[name].append((p1 | pd, p2, rollx(p1 | pd, step), rollx(p2, step)))
        todo_all = todo_all | todo1 | todo2 | todod
    def node(m):
        return where((m & 0x0000FF00) != 0, const(1), zero) + where((m & 0x00FF0000) != 0, const(2), zero) + where(srl(m, 24) != 0, const(3), zero)

    tables = []
    for base, name in ((0, "up"), (S, "dn")):
        for s in range(S):
            code = node(C[name][s])
            for r in range(0, s - L + 1):
                same = (C[name][s] & U[name][r]) != 0
                code = where(same, const(4 + base + r), code)
            tables.append(code)
    for base, name in ((2 * S, "p"), (2 * S + NX, "m")):
        for i in range(NX):
            here, passing = X[name][i][0], X[name][i][1]
            code = node(here)
            for r in range(0, min(X0 + i - L + 1, S)):
                code = where((here & U["up"][r]) != 0, const(4 + r), code)
                code = where((here & U["dn"][r]) != 0, const(4 + S + r), code)
            for r in range(0, i - L + 1):
                code = where((passing & X[name][r][2]) != 0, const(4 + base + r), code)
            tables.append(code)
    places = []
    for dx, dz, n, bit in kids:
        code = where((dx == 0) & (dz == 0), n, const(-1))
        for r in range(S):
            code = where((dx == 0) & ((bit & U["up"][r]) != 0), const(4 + r), code)
            code = where((dx == 0) & ((bit & U["dn"][r]) != 0), const(4 + S + r), code)
        for r in range(NX):
            code = where(((dx == 3) & ((bit & X["p"][r][2]) != 0)) | ((dx == 2) & ((bit & X["p"][r][3]) != 0)), const(4 + 2 * S + r), code)
            code = where(((dx == 1) & ((bit & X["m"][r][2]) != 0)) | ((dx == 2) & ((bit & X["m"][r][3]) != 0)), const(4 + 2 * S + NX + r), code)
        places.append(code)
    return tables, places, todo_all


def plan_kernel(parents, routes):
    shape = (8, 128)
    lane = lax.broadcasted_iota(jnp.int32, shape, 1)
    row = (lane & 7)

    def rollx(value, by):
        return pltpu.roll(value, (8 * by) % 128, 1)

    def rollz(value, by):
        if by == 1:
            return jnp.where(row >= 1, pltpu.roll(value, 1, 1), pltpu.roll(value, 121, 1))
        return jnp.where(row < 7, pltpu.roll(value, 127, 1), pltpu.roll(value, 7, 1))

    def or_all(value):
        for by in (4, 2, 1):
            value = value | pltpu.roll(value, by, 0)
        return value

    def constant(value):
        return jnp.full(shape, value, jnp.int32)

    ops = (jnp.where, rollx, rollz, lax.shift_right_logical, or_all, constant, lane)
    kids = [parents[i : i + 8] for i in range(0, parents.shape[0], 8)]
    tables, places, left_over = plan_routes(kids, ops, SLOTS, LAG, X_START, X_SLOTS)
    bad = left_over != 0
    for i, table in enumerate(tables):
        routes[i : i + 1] = table[0:1]
    for i, place in enumerate(places):
        start = PLACE_ROW + 8 * i
        routes[start : start + 8] = jnp.maximum(place, 0)
        bad = bad | (place < 0)
    bad = jnp.max(jnp.where(bad, 1.0, 0.0), axis=1, keepdims=True)
    bad = jnp.max(bad, axis=0, keepdims=True)
    last = PLACE_ROW + parents.shape[0]
    routes[last : last + 1] = jnp.where(jnp.broadcast_to(bad, (1, 128)) > 0.0, 1, 0)


def find_routes(parents, devices):
    children = parents.shape[0] // devices
    lines = jnp.tile(parents.reshape(devices, children).T, (1, 128 // devices))
    routes = pl.pallas_call(
        plan_kernel,
        out_shape=jax.ShapeDtypeStruct((PLACE_ROW + children + 2, 128), jnp.int32),
        name="find_routes",
    )(lines)
    return routes, routes[PLACE_ROW + children, 0] == 0


def per_device(
    ssm_resident, ssm_nodes, conv_resident, conv_nodes, convbc_resident, convbc_nodes,
    kv_resident, kv_nodes, len_resident, len_nodes, parents, alive_flags, queries, new_kv,
    x_in, gate_in, bc_in, dt_in, conv_x_weight, conv_bc_weight, a_log, dt_bias, skip_gain, norm_gain,
):
    devices = lax.axis_size("dp")
    me = lax.axis_index("dp")
    ring = devices // COLUMNS
    child_dev = parents.shape[0] // devices

    grouped = parents.reshape(devices, child_dev)
    match = (grouped // NODE_DEV)[:, None, :] == jnp.arange(devices)[None, :, None]
    tab = jnp.max(jnp.where(match, (grouped % NODE_DEV)[:, None, :], 0), axis=2).reshape(-1)
    own = lax.dynamic_slice_in_dim(parents, me * child_dev, child_dev)
    child_src = own // NODE_DEV
    mine = child_src[None, :] == jnp.arange(devices)[:, None]
    number = jnp.arange(child_dev)[None, :]
    first = jnp.min(jnp.where(mine, number, child_dev - 1), axis=1)
    second = jnp.max(jnp.where(mine, number, 0), axis=1)
    child_which = jnp.sum(jnp.where(mine & (number > first[:, None]), 1, 0), axis=0)
    relative = (
        (child_src // ring - me // ring) % COLUMNS * ring + (child_src % ring - me % ring) % ring
    )
    spot = jnp.arange(devices)[None, :] == relative[:, None]
    place = jnp.sum(jnp.where(spot, jnp.asarray(Slots(ring).table())[None, :], 0), axis=1)
    plan = jnp.concatenate([tab, first, second, child_src, child_which, place]).astype(jnp.int32)
    turned = [jnp.transpose(a, (1, 0, 2)) for a in (conv_resident, convbc_resident, conv_nodes, convbc_nodes)]
    arrays = [
        ssm_nodes, ssm_resident, kv_nodes, kv_resident, queries, new_kv, x_in, gate_in, bc_in,
        jnp.transpose(dt_in, (1, 2, 0)), *turned, conv_x_weight, conv_bc_weight, norm_gain[None, :],
    ]
    scalars = [len_nodes, len_resident, alive_flags, a_log, dt_bias, skip_gain]
    peers = lax.axis_size("tensor")
    routes, fits = find_routes(parents, devices)

    def go(routed):
        return lambda p, r, s, a: tuple(run_round(p, r, s, a, ring, peers, routed))

    attn, ssm_out, new_ssm = lax.cond(fits, go(True), go(False), plan, routes, scalars, arrays)
    return attn, jnp.transpose(ssm_out, (1, 0, 2)), new_ssm


def solution(mesh):
    return jax.shard_map(
        per_device,
        mesh=mesh,
        in_specs=(
            P("dp", "tensor", None, None),
            P("dp", "tensor", None, None),
            P("dp", None, "tensor"),
            P("dp", None, "tensor"),
            P("dp", None, None),
            P("dp", None, None),
            P("dp", None, None, "tensor"),
            P("dp", None, None, "tensor"),
            P("dp"),
            P(),
            P(),
            P("dp"),
            P("dp", None, "tensor"),
            P("dp", None, None, "tensor"),
            P("dp", None, "tensor"),
            P("dp", None, "tensor"),
            P("dp", None, None),
            P("dp", None, "tensor"),
            P(None, "tensor"),
            P(),
            P("tensor"),
            P("tensor"),
            P("tensor"),
            P("tensor"),
        ),
        out_specs=(P("dp", None, "tensor"), P("dp", None, "tensor"), P("dp", "tensor", None, None)),
        check_vma=False,
    )
```

```python
import functools

import jax
import jax.numpy as jnp
import numpy as np
from jax import lax
from jax.experimental import pallas as pl
from jax.experimental.pallas import tpu as pltpu
from jax.sharding import PartitionSpec as P

HEAD = 128
SSM_HEAD = 64
STATE = 256
KERNEL = 4
STEPS = 4
INNER = 4096
EPSILON = 1e-05
NODE_DEV = 4
GROUP = 5
COLUMNS = 4
MESH = pl.DeviceIdType.MESH


class Slots:
    def __init__(self, ring):
        half = ring // 2
        self.ring, self.half = ring, half
        self.plus_direct, self.plus_transit = {0: 0}, {0: 1}
        self.minus_direct, self.minus_transit = {0: 0}, {}
        self.plus_group, self.minus_group = [(0, 2)], [(0, 1)]
        for k in range(1, half):
            start = 2 + 3 * (k - 1)
            self.plus_direct[k], self.plus_direct[ring - k], self.plus_transit[k] = start, start + 1, start + 2
            self.plus_group.append((start, 3))
            start = 1 + 3 * (k - 1)
            self.minus_direct[k], self.minus_direct[ring - k], self.minus_transit[ring - k] = start, start + 1, start + 2
            self.minus_group.append((start, 3))
        start = 2 + 3 * (half - 1)
        self.plus_direct[half] = start
        self.plus_group.append((start, 1))
        start = 1 + 3 * (half - 1)
        self.minus_direct[half], self.minus_transit[half] = start, start + 1
        self.minus_group.append((start, 2))
        self.sent = 3 * half
        self.plus = ring
        self.minus = ring + self.sent + half
        self.total = ring + 2 * (self.sent + half)

    def table(self):
        place = np.zeros((COLUMNS, self.ring), np.int32)
        for dz in range(self.ring):
            place[0, dz] = dz
            place[3, dz] = self.plus + self.plus_direct[dz]
            place[1, dz] = self.minus + self.minus_direct[dz]
            if dz < self.half:
                place[2, dz] = self.plus + self.sent + dz
            else:
                place[2, dz] = self.minus + self.sent + (self.ring - dz) - 1
        return place.reshape(-1)


PAIR = 64
BACK = 48
BLOCK = 32
PAIR_DEVICES = 32
RING_GROUPS = 2
ROUTE_HEADS = (2, 2, 2, 2)

SLOTS, X_SLOTS, X_START, LAG = 12, 11, 7, 3
REPLY = 0
STRIDE = 12
PLACE_ROW = 2 * (SLOTS + X_SLOTS)
SRC_ROW, WHICH_ROW, FITS_ROW, PAIR_ROW = PLACE_ROW + 16, PLACE_ROW + 32, PLACE_ROW + 48, PLACE_ROW + 56


def dot(a, b, dims):
    return lax.dot_general(a, b, (dims, ((), ())), preferred_element_type=jnp.float32)


def silu(value):
    return value / (1.0 + jnp.exp(-value))


def softplus(value):
    return jnp.maximum(value, 0.0) + jnp.log1p(jnp.exp(-jnp.abs(value)))


def split(value, parts):
    pieces = []
    for _ in range(parts):
        piece = value.astype(jnp.bfloat16).astype(jnp.float32)
        pieces.append(piece)
        value = value - piece
    return pieces


def round_kernel(
    slots, heads, res_rows, child_dev, peers, routed,
    plan, routes, len_nodes, len_res, alive, a_log, dt_bias, skip_gain,
    ssm_h, res_h, kvn_h, kvr_h, q_h, nkv_h, x_h, g_h, bc_h, dt_h, cr_h, cbr_h, cn_h, cbn_h, wx_h, wbc_h, gain_h,
    att, ssm_out, new_out,
    *scratch,
):
    scratch = list(scratch)

    def take(count):
        taken, scratch[:count] = scratch[:count], []
        return taken

    loaded = take(17)
    (ssm, res, kv_nodes, kv_res, q_v, nkv_v, x_v, g_v, bc_v, dt_v, cr_v, cbr_v, cn_v, cbn_v, wx_v, wbc_v, gain_v) = loaded
    (load_sem,) = take(1)
    comb, convp, new_v, gather, shift, bias = take(6)
    ux, ub, c_parts, b_parts, w_parts, carried, rest, read = take(8)
    q_out, q_in, o_out, o_in = take(4)
    qsend, qrecv, rsend, rrecv = take(4)
    sums, landed, psend, precv = take(4)
    (new_sem,) = take(1)

    ring, half = slots.ring, slots.half
    groups = len(ROUTE_HEADS) if routed else RING_GROUPS
    devices = COLUMNS * ring
    rows = res_rows + child_dev
    features = heads * SSM_HEAD
    me = lax.axis_index("dp")
    tensor = lax.axis_index("tensor")
    x, z = me // ring, me % ring
    first_at = devices * devices
    second_at = first_at + devices
    src_at = second_at + devices
    which_at = src_at + child_dev
    place_at = which_at + child_dev

    sources = (ssm_h, res_h, kvn_h, kvr_h, q_h, nkv_h, x_h, g_h, bc_h, dt_h, cr_h, cbr_h, cn_h, cbn_h, wx_h, wbc_h, gain_h)
    loads = [pltpu.make_async_copy(a, b, load_sem.at[i]) for i, (a, b) in enumerate(zip(sources, loaded))]
    for load in loads:
        load.start()

    barrier = pltpu.get_barrier_semaphore()

    @pl.loop(1, devices)
    def _(step):
        pl.semaphore_signal(
            barrier, inc=1, device_id=((me + step) % devices, tensor), device_id_type=MESH
        )

    if peers > 1:

        @pl.loop(1, peers)
        def _(step):
            pl.semaphore_signal(
                barrier, inc=1, device_id=(me, (tensor + step) % peers), device_id_type=MESH
            )

    for load in loads:
        load.wait()

    def at(column, row):
        return ((column + COLUMNS) % COLUMNS) * ring + (row + ring) % ring

    above, below = at(x, z + 1), at(x, z - 1)
    right, left = at(x + 1, z), at(x - 1, z)
    across = at(x + 2, z)

    for node in range(NODE_DEV):
        lines = []
        for value in (cn_v, cbn_v):
            for j in range(KERNEL - 1):
                for begin in range(0, value.shape[2], STATE):
                    lines.append(value[j].astype(jnp.float32)[node : node + 1, begin : begin + STATE])
        used = len(lines)
        lines.append(jnp.zeros((16 - used, STATE), jnp.float32))
        convp[node, 0] = jnp.concatenate(lines, 0).astype(jnp.bfloat16)
    x_lines = (KERNEL - 1) * features // STATE

    pl.semaphore_wait(barrier, devices - 1 + peers - 1)

    def send(source, target, send_sem, recv_sem, device):
        return pltpu.make_async_remote_copy(
            src_ref=source,
            dst_ref=target,
            send_sem=send_sem,
            recv_sem=recv_sem,
            device_id=(device, tensor),
            device_id_type=MESH,
        )

    class Stream:
        def __init__(self, own, base, refs):
            self.own, self.base, self.count = own, base, refs[0].shape[0]
            (self.gz, self.sp, self.sm, self.arr,
             self.zsend, self.zrecv, self.xsend, self.xrecv, self.fsend, self.frecv) = refs

        def hop(self, c, k, up):
            if k == 1:
                source = self.own.at[:, self.base + c]
            else:
                source = self.gz.at[c, (ring - k + 1 if up else k - 1) - 1]
            target = self.gz.at[c, (ring - k if up else k) - 1]
            if k == half:
                nodes = pl.ds(0 if up else NODE_DEV // 2, NODE_DEV // 2)
                source, target = source.at[nodes], target.at[nodes]
            way = 0 if up else 1
            return send(
                source, target, self.zsend.at[c, way, k - 1], self.zrecv.at[c, way, k - 1],
                above if up else below,
            )

        def across_x(self, c, k, plus):
            start, size = (slots.plus_group if plus else slots.minus_group)[k]
            base = slots.plus if plus else slots.minus
            way = 0 if plus else 1
            return send(
                (self.sp if plus else self.sm).at[c, pl.ds(start, size)],
                self.arr.at[c, pl.ds(base + start, size)],
                self.xsend.at[c, way, k], self.xrecv.at[c, way, k],
                right if plus else left,
            )

        def forward(self, c, k, plus):
            if plus:
                source = slots.plus + slots.plus_transit[k]
                target = slots.plus + slots.sent + k
                index = k
            else:
                source = slots.minus + slots.minus_transit[half if k == half else ring - k]
                target = slots.minus + slots.sent + k - 1
                index = k - 1
            way = 0 if plus else 1
            return send(
                self.arr.at[c, source], self.arr.at[c, target],
                self.fsend.at[c, way, index], self.frecv.at[c, way, index],
                right if plus else left,
            )

        def pick(self, c, dz, target):
            node = plan[target * devices + at(x, z + dz)]
            if dz == 0:
                return self.own[node, self.base + c]
            picked = self.gz[c, dz - 1, 0]
            for other in range(1, NODE_DEV):
                picked = jnp.where(node == other, self.gz[c, dz - 1, other], picked)
            return picked

        def group(self, c, k):
            dzs = [0] if k == 0 else [half] if k == half else [k, ring - k]
            for dz in dzs:
                self.sp[c, slots.plus_direct[dz]] = self.pick(c, dz, right)
                self.sm[c, slots.minus_direct[dz]] = self.pick(c, dz, left)
                if dz in slots.plus_transit:
                    self.sp[c, slots.plus_transit[dz]] = self.pick(c, dz, across)
                else:
                    self.sm[c, slots.minus_transit[dz]] = self.pick(c, dz, across)
            self.across_x(c, k, True).start()
            self.across_x(c, k, False).start()
            for dz in dzs:
                self.arr[c, dz] = self.pick(c, dz, me)

        def stage(self, c, k):
            for up in (True, False):
                if k >= 1:
                    self.hop(c, k, up).wait_recv()
                if k < half:
                    self.hop(c, k + 1, up).start()
            self.group(c, k)

        def relay(self, c, k):
            for plus in (True, False):
                self.across_x(c, k, plus).wait_recv()
                if k in (range(half) if plus else range(1, half + 1)):
                    self.forward(c, k, plus).start()

        def arrive(self, c):
            for k in range(half + 1):
                for plus in (True, False):
                    if k in (range(half) if plus else range(1, half + 1)):
                        self.forward(c, k, plus).wait_recv()

        def finish(self, c):
            for k in range(1, half + 1):
                for up in (True, False):
                    self.hop(c, k, up).wait_send()
            for k in range(half + 1):
                for plus in (True, False):
                    self.across_x(c, k, plus).wait_send()
                    if k in (range(half) if plus else range(1, half + 1)):
                        self.forward(c, k, plus).wait_send()

    class Route:
        def __init__(self, own, base, count, refs):
            self.own, self.base, self.count = own, base, count
            self.inn, self.out, self.zsend, self.zrecv, self.xsend, self.xrecv = refs

        def copy(self, way, slot):
            start = (0, SLOTS, 2 * SLOTS, 2 * SLOTS + X_SLOTS)[way]
            if way < 2:
                sems = self.zsend.at[way, slot], self.zrecv.at[way, slot]
            else:
                sems = self.xsend.at[way - 2, slot], self.xrecv.at[way - 2, slot]
            return send(
                self.out.at[start + slot], self.inn.at[start + slot], *sems,
                (above, below, right, left)[way],
            )

        def first(self, code):
            node = jnp.minimum(code, NODE_DEV - 1)
            return tuple(self.own[node, self.base + h] for h in range(self.count))

        def choose(self, code, slot, held):
            return tuple(
                jnp.where(code == NODE_DEV + slot, self.inn[slot, h], held[h]) for h in range(self.count)
            )

        def put(self, way, slot, value):
            start = (0, SLOTS, 2 * SLOTS, 2 * SLOTS + X_SLOTS)[way]
            for h in range(self.count):
                self.out[start + slot, h] = value[h]
            self.copy(way, slot).start()

        def z_step(self, step):
            landed = step - LAG

            @pl.when((landed >= 0) & (landed < SLOTS))
            def _():
                for way in (0, 1):
                    self.copy(way, landed).wait_recv()

            @pl.when((step >= 0) & (step < SLOTS))
            def _():
                for way in (0, 1):
                    code = routes[way * SLOTS + step, me]
                    value = lax.fori_loop(
                        0, jnp.maximum(step - LAG + 1, 0),
                        lambda r, held: self.choose(code, way * SLOTS + r, held), self.first(code),
                    )
                    self.put(way, step, value)

        def x_step(self, step):
            slot = step - X_START
            landed = slot - LAG

            @pl.when((landed >= 0) & (landed < X_SLOTS))
            def _():
                for way in (2, 3):
                    self.copy(way, landed).wait_recv()

            @pl.when((slot >= 0) & (slot < X_SLOTS))
            def _():
                codes = [routes[2 * SLOTS + i * X_SLOTS + slot, me] for i in range(2)]

                def from_z(r, held):
                    result = []
                    for code, value in zip(codes, held):
                        for start in (0, SLOTS):
                            value = self.choose(code, start + r, value)
                        result.append(value)
                    return tuple(result)

                def from_x(r, held):
                    return tuple(
                        self.choose(codes[i], 2 * SLOTS + i * X_SLOTS + r, held[i]) for i in range(2)
                    )

                held = tuple(self.first(code) for code in codes)
                held = lax.fori_loop(0, jnp.minimum(step - LAG + 1, SLOTS), from_z, held)
                held = lax.fori_loop(0, jnp.maximum(landed + 1, 0), from_x, held)
                for i in range(2):
                    self.put(2 + i, slot, held[i])

        def arrived(self, child):
            code = routes[PLACE_ROW + child, me]
            slot = jnp.maximum(code - NODE_DEV, 0)
            held = self.first(code)
            return [jnp.where(code < NODE_DEV, held[h], self.inn[slot, h]) for h in range(self.count)]

        def finish(self, _):
            @pl.loop(0, SLOTS)
            def _(slot):
                for way in (0, 1):
                    self.copy(way, slot).wait_send()

            @pl.loop(0, X_SLOTS)
            def _(slot):
                for way in (2, 3):
                    self.copy(way, slot).wait_send()

    per_group = heads // groups
    if routed:
        main = [Route(ssm, sum(ROUTE_HEADS[:i]), ROUTE_HEADS[i], take(6)) for i in range(groups)]
        side = Route(convp, 0, 1, take(6))
    else:
        main = [Stream(ssm, i * per_group, take(10)) for i in range(groups)]
        side = Stream(convp, 0, take(10))

    def on_head(tick, offset, act):
        c = tick - offset
        for i in range(groups):

            @pl.when((c >= i * per_group) & (c < (i + 1) * per_group))
            def _():
                act(main[i], c - i * per_group)

    def weigh(weights, values):
        high = weights.astype(jnp.bfloat16)
        low = (weights - high.astype(jnp.float32)).astype(jnp.bfloat16)
        return dot(high, values, ((1,), (0,))) + dot(low, values, ((1,), (0,)))

    def attend(message, keys, values, length):
        scale = HEAD**-0.5
        old = dot(message, keys, ((1,), (1,))) * scale
        spot = lax.broadcasted_iota(jnp.int32, old.shape, 1)
        old = jnp.where(spot < length, old, -jnp.inf)
        moved = dot(shift[...], message, ((1,), (0,))).astype(jnp.bfloat16)
        new = dot(message, moved, ((1,), (1,))) * scale + bias[...]
        top = jnp.maximum(jnp.max(old, 1, keepdims=True), jnp.max(new, 1, keepdims=True))
        old, new = jnp.exp(old - top), jnp.exp(new - top)
        total = jnp.sum(old, 1, keepdims=True) + jnp.sum(new, 1, keepdims=True)
        return (weigh(old, values) + weigh(new, message)) / total

    def pack(first, second):
        both = jnp.concatenate([comb[first], comb[second]], 0)
        return dot(gather[...], both, ((1,), (0,))).astype(jnp.bfloat16)

    def asking(d):
        return send(q_out.at[d], q_in.at[me], qsend.at[d], qrecv.at[me], d)

    def asked(d):
        return send(q_out.at[d], q_in.at[d], qsend.at[d], qrecv.at[d], d)

    def reply(d):
        return send(o_out.at[d], o_in.at[me], rsend.at[d], rrecv.at[me], d)

    def replied(d):
        return send(o_out.at[d], o_in.at[d], rsend.at[d], rrecv.at[d], d)

    def prepare():
        r = lax.broadcasted_iota(jnp.int32, (PAIR, PAIR), 0)
        c = lax.broadcasted_iota(jnp.int32, (PAIR, PAIR), 1)
        query = r + jnp.where(r >= 20, 12, 0)
        key = r - 20 + jnp.where(r >= 44, 28, 0)
        value = r - 24 + jnp.where(r >= 52, 28, 0)
        column = jnp.where(r < 40, query, jnp.where(r < 48, key, jnp.where(r < 56, value, -1)))
        gather[...] = jnp.where(column == c, 1.0, 0.0).astype(jnp.bfloat16)
        shift[...] = jnp.where((r >= 48) & (r < 56) & (c == r - 8), 1.0, 0.0).astype(jnp.bfloat16)
        same = jnp.where(c >= 52, 1, 0) == jnp.where(r >= 20, 1, 0)
        seen = (r < 40) & (c >= 48) & (c < 56) & same & ((c & 3) <= (r & 3))
        bias[...] = jnp.where(seen, 0.0, -jnp.inf)

        @pl.loop(0, rows)
        def _(row):
            query = q_v[row].astype(jnp.float32)
            lines = [query[:, g * HEAD : (g + 1) * HEAD] for g in range(GROUP)]
            fresh = nkv_v[row].astype(jnp.float32)
            lines += [fresh[0], fresh[1], jnp.zeros((4, HEAD), jnp.float32)]
            comb[row] = jnp.concatenate(lines, 0).astype(jnp.bfloat16)

    def ask(steps):
        messages = []
        for step in steps:
            d = (me + step) % devices
            if routed:
                first, second = routes[PAIR_ROW + devices + d, me], routes[PAIR_ROW + 2 * devices + d, me]
            else:
                first, second = plan[first_at + d], plan[second_at + d]
            messages.append(pack(res_rows + first, res_rows + second))
        for step, message in zip(steps, messages):
            d = (me + step) % devices

            @pl.when(step == 0)
            def _():
                q_in[me] = message

            @pl.when(step != 0)
            def _():
                q_out[d] = message
                asking(d).start()

    def serve(steps):
        served = [(me + devices - step) % devices for step in steps]
        for step, d in zip(steps, served):

            @pl.when(step != 0)
            def _():
                asked(d).wait_recv()

        results = []
        for d in served:
            node = routes[PAIR_ROW + me, d] if routed else plan[d * devices + me]
            length = len_nodes[me * NODE_DEV + node]
            result = attend(q_in[d], kv_nodes[node, 0], kv_nodes[node, 1], length)
            results.append(result[:BACK].astype(jnp.bfloat16))
        for step, d, result in zip(steps, served, results):

            @pl.when(step == 0)
            def _():
                o_in[me] = result

            @pl.when(step != 0)
            def _():
                o_out[d] = result
                if not routed:
                    reply(d).start()

    def put_attended(row, value):
        value = jnp.where(alive[row] > 0, value, 0.0).astype(jnp.bfloat16)
        for g in range(GROUP):
            att[row, :, g * HEAD : (g + 1) * HEAD] = value[4 * g : 4 * g + 4]

    def resident(lines):
        messages = [pack(row, row) for row in lines]
        results = [
            attend(message, kv_res[row, 0], kv_res[row, 1], len_res[row])[:20]
            for row, message in zip(lines, messages)
        ]
        for row, result in zip(lines, results):
            put_attended(row, result)

    def convolve():
        for j in range(KERNEL - 1):
            ux[j, 0:res_rows] = cr_v[j].astype(jnp.float32)
            ub[j, 0:res_rows] = cbr_v[j].astype(jnp.float32)
        for child in range(child_dev):
            if routed:
                lines = side.arrived(child)[0].astype(jnp.float32)
            else:
                lines = side.arr[0, plan[place_at + child]].astype(jnp.float32)
            at_row = slice(res_rows + child, res_rows + child + 1)
            line = 0
            for target in (ux, ub):
                for j in range(KERNEL - 1):
                    for begin in range(0, target.shape[2], STATE):
                        target[j, at_row, begin : begin + STATE] = lines[line : line + 1]
                        line += 1
        fresh_x = x_v[...].astype(jnp.float32)
        fresh_b = bc_v[...].astype(jnp.float32)
        for t in range(STEPS):
            ux[KERNEL - 1 + t] = fresh_x[:, t, :]
            ub[KERNEL - 1 + t] = fresh_b[:, t, :]
        weights_x = wx_v[...].astype(jnp.float32)
        weights_b = wbc_v[...].astype(jnp.float32)

        def mix(source, weights, t):
            total = weights[0:1] * source[t]
            for tap in range(1, KERNEL):
                total = total + weights[tap : tap + 1] * source[t + tap]
            return silu(total)

        lane = lax.broadcasted_iota(jnp.int32, (1, features), 1)

        def spread(table):
            value = jnp.zeros((1, features), jnp.float32)
            for h in range(heads):
                inside = (lane >= h * SSM_HEAD) & (lane < (h + 1) * SSM_HEAD)
                value = jnp.where(inside, table[h], value)
            return value

        rate, offset, skip = -jnp.exp(spread(a_log)), spread(dt_bias), spread(skip_gain)
        head = lax.broadcasted_iota(jnp.int32, (heads, features), 0) * SSM_HEAD
        lanes = lax.broadcasted_iota(jnp.int32, (heads, features), 1)
        one_hot = jnp.where((lanes >= head) & (lanes < head + SSM_HEAD), 1.0, 0.0).astype(jnp.bfloat16)
        b_list = []
        c_parts[...] = jnp.zeros(c_parts.shape, jnp.float32)
        b_parts[...] = jnp.zeros(b_parts.shape, jnp.float32)
        w_parts[...] = jnp.zeros(w_parts.shape, jnp.float32)
        since = []
        for t in range(STEPS):
            both = mix(ub, weights_b, t)
            b, c = both[:, :STATE], both[:, STATE:]
            b_list.append(b)
            for part, piece in enumerate(split(c, 3)):
                c_parts[part * 4 + t] = piece
            high, low = split(b, 2)
            b_parts[t], b_parts[4 + t], b_parts[8 + t] = high, low, high
            dt = softplus(dot(dt_v[t], one_hot, ((0,), (0,))) + offset)
            decay = jnp.exp(rate * dt)
            mixed = mix(ux, weights_x, t)
            carried[t] = decay if t == 0 else carried[t - 1] * decay
            since = [value * decay for value in since] + [dt * mixed]
            total = skip * mixed
            for s in range(t + 1):
                total = total + since[s] * jnp.sum(c * b_list[s], 1, keepdims=True)
            rest[t] = total
        for s in range(STEPS):
            high, low = split(since[s], 2)
            w_parts[s], w_parts[4 + s], w_parts[8 + s] = high, high, low

    def new_copy(row, i):
        span = pl.ds(main[i].base, main[i].count)
        return pltpu.make_async_copy(new_v.at[row, span], new_out.at[row, span], new_sem.at[row, i])

    def update(row, i, state):
        base, count = main[i].base, main[i].count
        span = slice(base * SSM_HEAD, (base + count) * SSM_HEAD)
        width = count * SSM_HEAD
        here = pl.ds(row, 1)
        state = state.reshape(width, STATE)
        c_row = c_parts[:, here, :].reshape(16, STATE).astype(jnp.bfloat16)
        b_row = b_parts[:, here, :].reshape(16, STATE).astype(jnp.bfloat16)
        window = span.start // STATE * STATE
        w_row = w_parts[:, here, window : max(window + STATE, span.stop)]
        w_row = w_row[:, :, span.start - window : span.stop - window].reshape(16, width).astype(jnp.bfloat16)
        got = dot(c_row, state, ((1,), (1,)))
        got = got[0:4] + got[4:8] + got[8:12]
        read[row, 0:STEPS, span] = got
        added = dot(w_row, b_row, ((0,), (0,)))
        last = carried[STEPS - 1 : STEPS, here, window : max(window + STATE, span.stop)]
        last = last.reshape(1, last.shape[2])[:, span.start - window : span.stop - window]
        for h in range(count):
            part = slice(h * SSM_HEAD, (h + 1) * SSM_HEAD)
            factor = last[:, h * SSM_HEAD : h * SSM_HEAD + 1]
            new = factor * state[part].astype(jnp.float32) + added[part]
            new_v[row, base + h] = new.astype(jnp.bfloat16)
    def update_resident(lines):
        for row in lines:
            for i in range(groups):
                update(row, i, res[row, main[i].base : main[i].base + main[i].count])
        for row in lines:
            for i in range(groups):
                new_copy(row, i).start()

    def update_child(children, i):
        for child in children:
            if routed:
                state = jnp.stack(main[i].arrived(child))
            else:
                state = main[i].arr[:, plan[place_at + child]]
            update(res_rows + child, i, state)
        for child in children:
            new_copy(res_rows + child, i).start()

    def spread_over(tick, start, per_tick, total, act):
        steps = -(-total // per_tick)

        @pl.when((tick >= start) & (tick < start + steps))
        def _():
            act([(tick - start) * per_tick + j for j in range(per_tick)])

    def reply_all():
        @pl.loop(1, devices)
        def _(step):
            reply((me + devices - step) % devices).start()

    def gather_replies():
        @pl.loop(1, devices)
        def _(step):
            replied((me + step) % devices).wait_recv()

        @pl.loop(0, child_dev)
        def _(child):
            if routed:
                source, which = routes[SRC_ROW + child, me], routes[WHICH_ROW + child, me]
            else:
                source, which = plan[src_at + child], plan[which_at + child]
            value = o_in[source].astype(jnp.float32)
            put_attended(res_rows + child, jnp.where(which == 1, value[20:40], value[0:20]))

    def run_ring():
        batch = 4
        begin = [2 * k for k in range(half + 1)]
        ticks = heads + begin[half] + 1
        ready = begin[half] + 2
        landed_at = per_group + begin[half] + 1
        share = -(-child_dev // (ticks - landed_at))

        @pl.loop(0, ticks)
        def _(tick):
            for k in range(half, -1, -1):

                @pl.when(tick == begin[k])
                def _():
                    side.stage(0, k)

                on_head(tick, begin[k], lambda stream, c: stream.stage(c, k))
            for k in range(half, -1, -1):

                @pl.when(tick == begin[k] + 1)
                def _():
                    side.relay(0, k)

                on_head(tick, begin[k] + 1, lambda stream, c: stream.relay(c, k))

            @pl.when(tick == 0)
            def _():
                prepare()
                pl.loop(0, devices)(lambda step: ask([step]))

            @pl.when(tick == 1)
            def _():
                @pl.loop(0, res_rows)
                def _(row):
                    resident([row])

            @pl.when((tick >= 2) & (tick < 2 + devices // batch))
            def _():
                @pl.loop(0, batch)
                def _(i):
                    serve([(tick - 2) * batch + i])

            @pl.when(tick == ready)
            def _():
                side.arrive(0)
                convolve()

                @pl.loop(0, res_rows)
                def _(row):
                    update_resident([row])

            if groups > 1:

                @pl.when(tick == landed_at)
                def _():
                    @pl.loop(0, per_group)
                    def _(c):
                        main[0].arrive(c)

                @pl.when(tick >= landed_at)
                def _():
                    @pl.loop(0, share)
                    def _(i):
                        child = (tick - landed_at) * share + i

                        @pl.when(child < child_dev)
                        def _():
                            update_child([child], 0)

        @pl.loop(0, per_group)
        def _(c):
            main[-1].arrive(c)

    def run_routes():
        span = X_START + X_SLOTS + LAG
        children = span + 1 + -(-res_rows // 2)
        serve_from = 8
        wait = -(-child_dev // 4)
        ticks = (groups - 1) * STRIDE + span

        @pl.loop(0, ticks)
        def _(tick):
            for i in range(groups):
                main[i].z_step(tick - i * STRIDE)
            side.z_step(tick)
            for i in range(groups):
                main[i].x_step(tick - i * STRIDE)
            side.x_step(tick)
            pl.when(tick == 0)(prepare)
            spread_over(tick, 1, 1, devices, ask)
            spread_over(tick, 9, 4, res_rows, resident)
            spread_over(tick, serve_from, 1, devices, serve)
            pl.when(tick == span)(convolve)
            spread_over(tick, span + 1, 2, res_rows, update_resident)
            for i in range(groups - 1):
                start = max(children + i * wait, i * STRIDE + span)
                spread_over(tick, start, 4, child_dev, functools.partial(update_child, i=i))
            pl.when(tick == ticks - span + SLOTS + REPLY)(reply_all)

    if routed:
        run_routes()
    else:
        run_ring()

    @pl.loop(0, child_dev // 4)
    def _(part):
        update_child([4 * part + j for j in range(4)], groups - 1)

    gated = []
    gates = g_v[...].astype(jnp.float32)
    reads = read[...]
    lane = lax.broadcasted_iota(jnp.int32, (rows, 128), 1)
    total = jnp.zeros((rows, 128), jnp.float32)
    for t in range(STEPS):
        value = (carried[t] * reads[:, t, :] + rest[t]) * silu(gates[:, t, :])
        gated.append(value)
        total = jnp.where(lane == t, jnp.sum(value * value, 1, keepdims=True), total)
    sums[...] = total

    def share_sums(d, slot):
        return pltpu.make_async_remote_copy(
            src_ref=sums, dst_ref=landed.at[slot], send_sem=psend.at[d], recv_sem=precv.at[slot],
            device_id=(me, d), device_id_type=MESH,
        )

    if peers > 1:

        @pl.loop(1, peers)
        def _(step):
            share_sums((tensor + step) % peers, tensor).start()

    gather_replies()
    for stream, count in [(side, 1)] + [(m, 1 if routed else per_group) for m in main]:

        @pl.loop(0, count)
        def _(c):
            stream.finish(c)

    @pl.loop(1, devices)
    def _(step):
        d = (me + step) % devices
        asking(d).wait_send()
        reply(d).wait_send()

    if peers > 1:

        @pl.loop(1, peers)
        def _(step):
            d = (tensor + step) % peers
            share_sums(d, d).wait_recv()

        landed[tensor] = sums[...]
        total = landed[0]
        for d in range(1, peers):
            total = total + landed[d]
    scale = lax.rsqrt(total / INNER + EPSILON)
    row_of = lax.broadcasted_iota(jnp.int32, (rows, 128), 0)
    living = jnp.zeros((rows, 128), jnp.int32)
    for row in range(rows):
        living = jnp.where(row_of == row, alive[row], living)
    for t in range(STEPS):
        result = gated[t] * scale[:, t : t + 1] * gain_v[...]
        ssm_out[t] = jnp.where(living[:, 0:1] > 0, result, 0.0).astype(jnp.bfloat16)

    @pl.loop(0, rows)
    def _(row):
        for i in range(groups):
            new_copy(row, i).wait()

    if peers > 1:

        @pl.loop(1, peers)
        def _(step):
            share_sums((tensor + step) % peers, tensor).wait_send()


def run_round(plan, routes, scalars, arrays, ring, peers, routed):
    slots = Slots(ring)
    half = ring // 2
    devices = COLUMNS * ring
    ssm, res, queries, gate = arrays[0], arrays[1], arrays[4], arrays[7]
    heads = ssm.shape[1]
    rows, res_rows = queries.shape[0], res.shape[0]
    child_dev = rows - res_rows
    features = heads * SSM_HEAD
    groups = len(ROUTE_HEADS) if routed else RING_GROUPS
    per_group = heads // groups
    bf16, f32 = jnp.bfloat16, jnp.float32
    dma = pltpu.SemaphoreType.DMA

    def stream(count, height):
        return [
            pltpu.VMEM((count, ring - 1, NODE_DEV, height, STATE), bf16),
            pltpu.VMEM((count, slots.sent, height, STATE), bf16),
            pltpu.VMEM((count, slots.sent, height, STATE), bf16),
            pltpu.VMEM((count, slots.total, height, STATE), bf16),
            dma((count, 2, half)), dma((count, 2, half)),
            dma((count, 2, half + 1)), dma((count, 2, half + 1)),
            dma((count, 2, half)), dma((count, 2, half)),
        ]

    scratch = [pltpu.VMEM(a.shape, a.dtype) for a in arrays] + [dma((len(arrays),))]
    scratch += [
        pltpu.VMEM((rows, BLOCK, HEAD), bf16),
        pltpu.VMEM((NODE_DEV, 1, 16, STATE), bf16),
        pltpu.VMEM((rows, heads, SSM_HEAD, STATE), bf16),
        pltpu.VMEM((PAIR, PAIR), bf16),
        pltpu.VMEM((PAIR, PAIR), bf16),
        pltpu.VMEM((PAIR, PAIR), f32),
    ]
    taps = KERNEL - 1 + STEPS
    scratch += [
        pltpu.VMEM((taps, rows, features), f32),
        pltpu.VMEM((taps, rows, 2 * STATE), f32),
        pltpu.VMEM((16, rows, STATE), f32),
        pltpu.VMEM((16, rows, STATE), f32),
        pltpu.VMEM((16, rows, features), f32),
        pltpu.VMEM((STEPS, rows, features), f32),
        pltpu.VMEM((STEPS, rows, features), f32),
        pltpu.VMEM((rows, 8, features), f32),
    ]
    scratch += [
        pltpu.VMEM((devices, PAIR, HEAD), bf16),
        pltpu.VMEM((devices, PAIR, HEAD), bf16),
        pltpu.VMEM((devices, BACK, HEAD), bf16),
        pltpu.VMEM((devices, BACK, HEAD), bf16),
    ] + [dma((devices,))] * 4
    scratch += [
        pltpu.VMEM((rows, 128), f32),
        pltpu.VMEM((peers, rows, 128), f32),
        dma((peers,)),
        dma((peers,)),
        dma((rows, groups)),
    ]
    def route(count, height):
        packets = 2 * (SLOTS + X_SLOTS)
        return [
            pltpu.VMEM((packets, count, height, STATE), bf16),
            pltpu.VMEM((packets, count, height, STATE), bf16),
            dma((2, SLOTS)), dma((2, SLOTS)), dma((2, X_SLOTS)), dma((2, X_SLOTS)),
        ]

    for _ in range(groups):
        scratch += route(ROUTE_HEADS[_], SSM_HEAD) if routed else stream(per_group, SSM_HEAD)
    scratch += (route if routed else stream)(1, 16)
    smem = pl.BlockSpec(memory_space=pltpu.SMEM)
    vmem = pl.BlockSpec(memory_space=pltpu.VMEM)
    anywhere = pl.BlockSpec(memory_space=pl.ANY)
    return pl.pallas_call(
        functools.partial(round_kernel, slots, heads, res_rows, child_dev, peers, routed),
        out_shape=[
            jax.ShapeDtypeStruct(queries.shape, bf16),
            jax.ShapeDtypeStruct((STEPS, rows, features), bf16),
            jax.ShapeDtypeStruct((rows,) + ssm.shape[1:], bf16),
        ],
        in_specs=[smem] * (2 + len(scalars)) + [anywhere] * len(arrays),
        out_specs=[vmem, vmem, anywhere],
        scratch_shapes=scratch,
        compiler_params=pltpu.CompilerParams(
            collective_id=1 if routed else 0, has_side_effects=True, vmem_limit_bytes=60 * 1024 * 1024
        ),
        name="routed_round" if routed else "ring_round",
    )(plan, routes, *scalars, *arrays)


def plan_routes(parents, ops, S, L, X0, NX):
    where, rollx, rollz, srl, orall, const, lanes = ops
    x, z = (lanes >> 3) & 3, lanes & 7
    kids = []
    zero = const(0)
    need = [zero, zero, zero, zero]
    for p in parents:
        src, n = p >> 2, p & 3
        dx, dz = ((src >> 3) - x) & 3, ((src & 7) - z) & 7
        bit = const(1) << (n * 8 + dz)
        kids.append((dx, dz, n, bit))
        for k in range(4):
            need[k] = need[k] | where(dx == k, bit, zero)
    need = [orall(v) for v in need]
    me_, across, right, left = need[0], rollx(need[2], 2), rollx(need[3], -1), rollx(need[1], 1)
    row = me_ | across | right | left
    D4, D5, D3 = 0x10101010, 0x20202020, 0x08080808
    UPB, DNB = 0xE0E0E0E0 - (1 << 32), 0x0E0E0E0E
    D0 = 0x01010101
    ev = 0x00100010
    opp = row & D4
    up_near, dn_near = zero, zero
    go_up, go_dn = zero, zero
    from_below, from_above = row, row
    for k in (1, 2, 3):
        from_below, from_above = rollz(from_below, 1), rollz(from_above, -1)
        up_near = up_near | (srl(from_below, k) & opp)
        dn_near = dn_near | ((from_above << k) & opp)
        go_up = go_up | (up_near & ~dn_near)
        go_dn = go_dn | (dn_near & ~up_near)
    go_up = go_up | (opp & ~go_dn & ev)
    need_up = (row & UPB) | go_up
    need_dn = (row & DNB) | (opp & ~go_up)

    def sender_up(m):
        return srl(m & (0x80808080 - (1 << 32)), 7) & D0 | ((m & 0x70707070) << 1)

    def receiver_up(m):
        return ((m & D0) << 7) | srl(m & UPB, 1)

    def sender_dn(m):
        return srl(m & (DNB | D4), 1)

    def receiver_dn(m):
        return m << 1

    todo_all = zero
    C, U = {}, {}
    for name, wanted, step, send, recv, keep in (
        ("up", need_up, 1, sender_up, receiver_up, UPB),
        ("dn", need_dn, -1, sender_dn, receiver_dn, DNB),
    ):
        A = [send(rollz(wanted, -step))]
        for _ in range(3):
            A.append(send(rollz(A[-1] & keep, -step)))
        act = A[0] | A[1] | A[2] | A[3]
        ready = act & D0
        todo = act
        come = {}
        C[name], U[name] = [], []
        for s in range(S):
            if s in come:
                ready = ready | (come[s] & act)
            best = ready & A[3]
            for k in (2, 1, 0):
                best = where(best != 0, best, ready & A[k])
            pick = best & -best
            ready = ready & ~pick
            todo = todo & ~pick
            got = rollz(recv(pick), step)
            C[name].append(pick)
            U[name].append(got)
            come[s + L] = got
        todo_all = todo_all | todo
    EVEN = 0x55555555
    first_p = (across & right) | (across & ~left & EVEN)
    first_m = across & ~first_p
    direct_p, direct_m = right & ~first_p, left & ~first_m
    X = {}
    for name, step, direct, first in (("p", 1, direct_p, first_p), ("m", -1, direct_m, first_m)):
        arrived = {}
        second = rollx(first, step)
        todo1, todo2, todod = first, second, direct
        have = D0 | zero
        got2 = zero
        come = {}
        X[name] = []
        for t in range(X0 + NX):
            s = t - L
            if 0 <= s < S:
                have = have | U["up"][s] | U["dn"][s]
            if t in come:
                got2 = got2 | come[t]
            if t < X0:
                continue
            r1, r2, rd = todo1 & have, todo2 & got2, todod & have
            p1 = r1 & -r1
            none = r1 == 0
            p2 = where(none, r2 & -r2, zero)
            none = none & (r2 == 0)
            pd = where(none, rd & -rd, zero)
            todo1, todo2, todod = todo1 & ~p1, todo2 & ~p2, todod & ~pd
            come[t + L] = rollx(p1, step)
            X[name].append((p1 | pd, p2, rollx(p1 | pd, step), rollx(p2, step)))
        todo_all = todo_all | todo1 | todo2 | todod
    def node(m):
        return where((m & 0x0000FF00) != 0, const(1), zero) + where((m & 0x00FF0000) != 0, const(2), zero) + where(srl(m, 24) != 0, const(3), zero)

    tables = []
    for base, name in ((0, "up"), (S, "dn")):
        for s in range(S):
            code = node(C[name][s])
            for r in range(0, s - L + 1):
                same = (C[name][s] & U[name][r]) != 0
                code = where(same, const(4 + base + r), code)
            tables.append(code)
    for base, name in ((2 * S, "p"), (2 * S + NX, "m")):
        for i in range(NX):
            here, passing = X[name][i][0], X[name][i][1]
            code = node(here)
            for r in range(0, min(X0 + i - L + 1, S)):
                code = where((here & U["up"][r]) != 0, const(4 + r), code)
                code = where((here & U["dn"][r]) != 0, const(4 + S + r), code)
            for r in range(0, i - L + 1):
                code = where((passing & X[name][r][2]) != 0, const(4 + base + r), code)
            tables.append(code)
    places = []
    for dx, dz, n, bit in kids:
        code = where((dx == 0) & (dz == 0), n, const(-1))
        for r in range(S):
            code = where((dx == 0) & ((bit & U["up"][r]) != 0), const(4 + r), code)
            code = where((dx == 0) & ((bit & U["dn"][r]) != 0), const(4 + S + r), code)
        for r in range(NX):
            code = where(((dx == 3) & ((bit & X["p"][r][2]) != 0)) | ((dx == 2) & ((bit & X["p"][r][3]) != 0)), const(4 + 2 * S + r), code)
            code = where(((dx == 1) & ((bit & X["m"][r][2]) != 0)) | ((dx == 2) & ((bit & X["m"][r][3]) != 0)), const(4 + 2 * S + NX + r), code)
        places.append(code)
    return tables, places, todo_all


def plan_kernel(parents, routes):
    shape = (8, 128)
    lane = lax.broadcasted_iota(jnp.int32, shape, 1)
    row = (lane & 7)

    def rollx(value, by):
        return pltpu.roll(value, (8 * by) % 128, 1)

    def rollz(value, by):
        if by == 1:
            return jnp.where(row >= 1, pltpu.roll(value, 1, 1), pltpu.roll(value, 121, 1))
        return jnp.where(row < 7, pltpu.roll(value, 127, 1), pltpu.roll(value, 7, 1))

    def or_all(value):
        for by in (4, 2, 1):
            value = value | pltpu.roll(value, by, 0)
        return value

    def constant(value):
        return jnp.full(shape, value, jnp.int32)

    ops = (jnp.where, rollx, rollz, lax.shift_right_logical, or_all, constant, lane)
    kids = [parents[i : i + 8] for i in range(0, parents.shape[0], 8)]
    tables, places, left_over = plan_routes(kids, ops, SLOTS, LAG, X_START, X_SLOTS)
    bad = left_over != 0
    for i, table in enumerate(tables):
        routes[i : i + 1] = table[0:1]
    for i, place in enumerate(places):
        start = PLACE_ROW + 8 * i
        routes[start : start + 8] = jnp.maximum(place, 0)
        bad = bad | (place < 0)
    bad = jnp.max(jnp.where(bad, 1.0, 0.0), axis=1, keepdims=True)
    bad = jnp.max(bad, axis=0, keepdims=True)
    routes[FITS_ROW : FITS_ROW + 8] = jnp.where(jnp.broadcast_to(bad, shape) > 0.0, 1, 0)

    def over(value, pick):
        for by in (4, 2, 1):
            value = pick(value, pltpu.roll(value, by, 0))
        return value

    line = lax.broadcasted_iota(jnp.int32, shape, 0)
    index = [line + 8 * i for i in range(len(kids))]
    which = [constant(0) for _ in kids]
    count = PAIR_DEVICES
    for source in range(count):
        here = [(kid >> 2) == source for kid in kids]

        def gather(values, other, pick):
            parts = [jnp.where(at, value, other) for at, value in zip(here, values)]
            return over(functools.reduce(pick, parts), pick)

        first = gather(index, 8 * len(kids) - 1, jnp.minimum)
        for i, value in enumerate((
            gather([kid & 3 for kid in kids], 0, jnp.maximum), first, gather(index, 0, jnp.maximum),
        )):
            at_row = PAIR_ROW + i * count + source
            routes[at_row : at_row + 1] = value[0:1]
        which = [jnp.where(at & (i > first), 1, w) for at, i, w in zip(here, index, which)]
    for i, kid in enumerate(kids):
        routes[SRC_ROW + 8 * i : SRC_ROW + 8 * i + 8] = kid >> 2
        routes[WHICH_ROW + 8 * i : WHICH_ROW + 8 * i + 8] = which[i]


def find_routes(parents, devices):
    children = parents.shape[0] // devices
    lines = jnp.tile(parents.reshape(devices, children).T, (1, 128 // devices))
    routes = pl.pallas_call(
        plan_kernel,
        out_shape=jax.ShapeDtypeStruct((PAIR_ROW + 3 * devices, 128), jnp.int32),
        name="find_routes",
    )(lines)
    return routes, routes[FITS_ROW, 0] == 0


def per_device(
    ssm_resident, ssm_nodes, conv_resident, conv_nodes, convbc_resident, convbc_nodes,
    kv_resident, kv_nodes, len_resident, len_nodes, parents, alive_flags, queries, new_kv,
    x_in, gate_in, bc_in, dt_in, conv_x_weight, conv_bc_weight, a_log, dt_bias, skip_gain, norm_gain,
):
    devices = lax.axis_size("dp")
    me = lax.axis_index("dp")
    ring = devices // COLUMNS
    child_dev = parents.shape[0] // devices

    def ring_plan(parents):
        grouped = parents.reshape(devices, child_dev)
        match = (grouped // NODE_DEV)[:, None, :] == jnp.arange(devices)[None, :, None]
        tab = jnp.max(jnp.where(match, (grouped % NODE_DEV)[:, None, :], 0), axis=2).reshape(-1)
        own = lax.dynamic_slice_in_dim(parents, me * child_dev, child_dev)
        child_src = own // NODE_DEV
        mine = child_src[None, :] == jnp.arange(devices)[:, None]
        number = jnp.arange(child_dev)[None, :]
        first = jnp.min(jnp.where(mine, number, child_dev - 1), axis=1)
        second = jnp.max(jnp.where(mine, number, 0), axis=1)
        child_which = jnp.sum(jnp.where(mine & (number > first[:, None]), 1, 0), axis=0)
        relative = (
            (child_src // ring - me // ring) % COLUMNS * ring + (child_src % ring - me % ring) % ring
        )
        spot = jnp.arange(devices)[None, :] == relative[:, None]
        place = jnp.sum(jnp.where(spot, jnp.asarray(Slots(ring).table())[None, :], 0), axis=1)
        return jnp.concatenate([tab, first, second, child_src, child_which, place]).astype(jnp.int32)

    turned = [jnp.transpose(a, (1, 0, 2)) for a in (conv_resident, convbc_resident, conv_nodes, convbc_nodes)]
    arrays = [
        ssm_nodes, ssm_resident, kv_nodes, kv_resident, queries, new_kv, x_in, gate_in, bc_in,
        jnp.transpose(dt_in, (1, 2, 0)), *turned, conv_x_weight, conv_bc_weight, norm_gain[None, :],
    ]
    scalars = [len_nodes, len_resident, alive_flags, a_log, dt_bias, skip_gain]
    peers = lax.axis_size("tensor")
    routes, fits = find_routes(parents, devices)

    def by_routes(p, r, s, a):
        return tuple(run_round(s[0], r, s, a, ring, peers, True))

    def by_ring(p, r, s, a):
        return tuple(run_round(ring_plan(p), r, s, a, ring, peers, False))

    attn, ssm_out, new_ssm = lax.cond(fits, by_routes, by_ring, parents, routes, scalars, arrays)
    return attn, jnp.transpose(ssm_out, (1, 0, 2)), new_ssm


def solution(mesh):
    return jax.shard_map(
        per_device,
        mesh=mesh,
        in_specs=(
            P("dp", "tensor", None, None),
            P("dp", "tensor", None, None),
            P("dp", None, "tensor"),
            P("dp", None, "tensor"),
            P("dp", None, None),
            P("dp", None, None),
            P("dp", None, None, "tensor"),
            P("dp", None, None, "tensor"),
            P("dp"),
            P(),
            P(),
            P("dp"),
            P("dp", None, "tensor"),
            P("dp", None, None, "tensor"),
            P("dp", None, "tensor"),
            P("dp", None, "tensor"),
            P("dp", None, None),
            P("dp", None, "tensor"),
            P(None, "tensor"),
            P(),
            P("tensor"),
            P("tensor"),
            P("tensor"),
            P("tensor"),
        ),
        out_specs=(P("dp", None, "tensor"), P("dp", None, "tensor"), P("dp", "tensor", None, None)),
        check_vma=False,
    )
```
